256 devices in a mesh: grp: 8 (over x, core), tbl: 32 (over y, z).
Axes of the slice: x: 4, y: 4, z: 8, core: 2. Of those that a mesh axis runs over, the one named last changes fastest.
Arguments:
- cross_input: bfloat16 [32768, 3456], P(('grp', 'tbl')), may hold values from -6 to 6
- upstream: bfloat16 [32768, 3456], P(('grp', 'tbl')), may hold values from -6 to 6
- v_weight: bfloat16 [256, 3456], replicated, may hold values from -0.109375 to 0.109375
- u_weight: bfloat16 [256, 3456], replicated, may hold values from -0.375 to 0.375
- bias: float32 [3456], replicated, may hold values from -3 to 3
- placement: int32 [26], replicated, may hold values from 0 to 31, as said below
- owned_ids: int32 [64, 4, 32768], P('tbl', None, 'grp'), may hold values from 0 to 255
Outputs:
- cross_grad: float32 [256, 6912], P(('grp', 'tbl'))
- table_grad: float32 [64, 256, 128], P('tbl', 'grp')
The draws below stay inside these ranges and needn't reach their ends.
Inputs may be any that keep to these rules, and one draw needn't show every extreme that they name: `placement`: no device holds more than 2 tables, and some device holds exactly 2.
All inputs are finite; a program needn't handle non-finite values.
Results may differ from the reference program's by a relative error of at most 0.004.
Values may be sent and summed in bfloat16 or wider, within the bound.
No kernel may reach another device: no remote copies, remote signals or barrier semaphores. Data moves between devices by JAX's collectives and lax.ppermute only.
A program may use at most 64 MiB of HBM per device.

```python
import math
import jax
import jax.numpy as jnp
import numpy as np
from jax import lax

EMB = 128
TABLES = 26
D = 3456
RANK = 256
TOK_DEV = 128
HOT = 4
ROWS = 256
MAXT = 2
SLOTS = 64
TOKENS = 32768
N_TBL = 32
DEVICES = 256


def draw_placement(key, part):
    key_heavy = jax.random.fold_in(key, 11)
    key_score = jax.random.fold_in(key, 12)
    key_order = jax.random.fold_in(key, 13)
    total = N_TBL * MAXT
    heavy = jax.random.randint(key_heavy, (), 0, N_TBL)
    score = jax.random.permutation(key_score, total).astype(jnp.int32)
    slot_ids = jnp.arange(total, dtype=jnp.int32)
    score = jnp.where(slot_ids // MAXT == heavy, total + slot_ids, score)
    unused, chosen = lax.top_k(score, TABLES)
    order = jax.random.permutation(key_order, TABLES)
    return (chosen // MAXT)[order].astype(jnp.int32)


def place_ends(result, own_key, low, high):
    dims = result.shape
    place = [jax.random.randint(jax.random.fold_in(own_key, axis), (), 0, dims[axis]) for axis in range(len(dims))]
    result = result.at[tuple(place)].set(low)
    longest = dims.index(max(dims))
    place[longest] = (place[longest] + 1) % dims[longest]
    return result.at[tuple(place)].set(high)


def level_of(rng, dims, pieces, smallest, top_value):
    level, own = 1.0, jax.random.fold_in(rng, 6)
    for dim, blocks in pieces:
        steps = jnp.exp(jax.random.uniform(jax.random.fold_in(own, dim), (blocks,), jnp.float32, smallest / len(pieces), top_value / len(pieces)))
        level = level * jnp.repeat(steps, dims[dim] // blocks).reshape([-1 if axis == dim else 1 for axis in range(len(dims))])
    return level


def rank_bounds(count, slope):
    portions = [(1 << 20) // math.isqrt(standing ** slope) + 1 for standing in range(1, count + 1)]
    spread = 1 + sum(portions) // (1 << 30)
    return np.cumsum(np.array([max(1, weight // spread) for weight in portions]))


def skewed_ids(rng, shape, number_of, slope):
    grid = rank_bounds(number_of, slope)
    pick = jax.random.randint(jax.random.fold_in(rng, 1), shape, 0, int(grid[number_of - 1]))
    standing = jnp.searchsorted(jnp.asarray(grid, jnp.int32), pick, side="right")
    return jax.random.permutation(jax.random.fold_in(rng, 2), number_of)[standing].astype(jnp.int32)


def centred(rng, shape, scale, bound, pieces=(), held_as=jnp.bfloat16):
    drawn = jax.random.normal(rng, shape, jnp.float32) * scale
    if len(pieces) > 0:
        drawn = level_of(rng, shape, pieces, -0.22, 0.18) * drawn
    return jnp.clip(drawn, min=-bound, max=bound).astype(held_as)


def setup_inputs(seed: int = 0) -> dict:
    streams_of = jax.random.split(jax.random.key(seed), 8)
    return {
        "cross_input": centred(streams_of[0], (TOKENS, D), 1.0, 6.0, ((0, 256),)),
        "upstream": centred(streams_of[1], (TOKENS, D), 1.0, 6.0, ((0, 256),)),
        "v_weight": centred(streams_of[2], (RANK, D), D ** -0.5, 0.109375),
        "u_weight": centred(streams_of[3], (RANK, D), RANK ** -0.5, 0.375),
        "bias": centred(streams_of[4], (D,), 0.5, 3.0, (), jnp.float32),
        "placement": draw_placement(jax.random.fold_in(streams_of[7], 71), 0),
        "owned_ids": place_ends(skewed_ids(streams_of[6], (SLOTS, HOT, TOKENS), ROWS, 1), jax.random.fold_in(streams_of[6], 3), 0, ROWS - 1).astype(jnp.int32),
    }


def block_terms(cross_input, upstream, v_weight, u_weight, bias):
    hidden = jnp.dot(cross_input, v_weight.T, preferred_element_type=jnp.float32).astype(jnp.bfloat16)
    mixed = jnp.dot(hidden, u_weight, preferred_element_type=jnp.float32) + bias
    up_float = upstream.astype(jnp.float32)
    product_grad = (up_float * cross_input.astype(jnp.float32)).astype(jnp.bfloat16)
    grad_u = jnp.dot(hidden.T, product_grad, preferred_element_type=jnp.float32)
    hidden_grad = jnp.dot(product_grad, u_weight.T, preferred_element_type=jnp.float32).astype(jnp.bfloat16)
    grad_v = jnp.dot(hidden_grad.T, cross_input, preferred_element_type=jnp.float32)
    input_grad = up_float * (1.0 + mixed) + jnp.dot(hidden_grad, v_weight, preferred_element_type=jnp.float32)
    pooled = input_grad[:, EMB:].astype(jnp.bfloat16)
    return (grad_u, grad_v, pooled)

def reference(cross_input, upstream, v_weight, u_weight, bias, placement, owned_ids):
    inputs_blocks = cross_input.reshape(DEVICES, TOK_DEV, D)
    upstream_blocks = upstream.reshape(DEVICES, TOK_DEV, D)

    def advance(carry, item):
        grad_u, grad_v, pooled = block_terms(item[0], item[1], v_weight, u_weight, bias)
        return ((carry[0] + grad_u, carry[1] + grad_v), pooled)
    start = (jnp.zeros((RANK, D), jnp.float32), jnp.zeros((RANK, D), jnp.float32))
    sums, pooled = lax.scan(advance, start, (inputs_blocks, upstream_blocks))
    cross_grad = jnp.concatenate([sums[0], sums[1]], axis=1) * (1.0 / math.sqrt(TOKENS))
    pooled = pooled.reshape(TOKENS, TABLES, EMB)
    same = placement[:, None] == placement[None, :]
    earlier = jnp.arange(TABLES)[None, :] < jnp.arange(TABLES)[:, None]
    slot = lax.optimization_barrier(jnp.sum((same & earlier).astype(jnp.int32), axis=1)).astype(jnp.int32)
    target = (placement * MAXT + slot).astype(jnp.int32)
    table_grad = jnp.zeros((SLOTS, ROWS, EMB), jnp.float32)
    for table in range(TABLES):
        values = pooled[:, table, :].astype(jnp.float32)
        row_ids = owned_ids[target[table]]
        total = jnp.zeros((ROWS, EMB), jnp.float32)
        for lookup in range(HOT):
            total = total + jax.ops.segment_sum(values, row_ids[lookup], num_segments=ROWS)
        table_grad = table_grad.at[target[table]].add(total)
    return (cross_grad, table_grad)
```

```python
import functools
import math

import jax
import jax.numpy as jnp
from jax import lax
from jax.experimental import pallas as pl
from jax.experimental.pallas import tpu as pltpu
from jax.sharding import Mesh
from jax.sharding import PartitionSpec as P

EMB = 128
TABLES = 26
ROWS = 256
RANK = 256
BF = jnp.bfloat16
F32 = jnp.float32


def nt(left, right):
    return lax.dot_general(left, right, (((1,), (1,)), ((), ())), preferred_element_type=F32)


def tn(left, right):
    return lax.dot_general(left, right, (((0,), (0,)), ((), ())), preferred_element_type=F32)


def own_rows(full, core):
    picks = [
        jnp.where(core == 0, full[i * 64 : i * 64 + 32], full[i * 64 + 32 : i * 64 + 64])
        for i in range(4)
    ]
    return jnp.concatenate(picks, axis=0)


def dense_kernel(meta, x, px, up, pup, v, u, hid_t, hgr_t, by_x, by_y, both, prod):
    core = meta[0]
    n = x.shape[0]
    both[:n] = x[...]
    both[n:] = px[...]
    prod[:n] = (x[...].astype(F32) * up[...].astype(F32)).astype(BF)
    prod[n:] = (px[...].astype(F32) * pup[...].astype(F32)).astype(BF)
    hid = nt(v[...], both[...])
    hgr = nt(u[...], prod[...])
    hid_t[...] = hid.astype(BF)
    hgr_t[...] = hgr.astype(BF)
    hid_own = own_rows(hid, core).astype(BF)
    hgr_own = own_rows(hgr, core).astype(BF)
    width = 1152
    for k in range(x.shape[1] // width):
        cols = slice(k * width, (k + 1) * width)
        first = jnp.dot(hid_own, prod[:, cols], preferred_element_type=F32)
        for i in range(4):
            by_x[i, :, cols] = first[i * 32 : (i + 1) * 32].astype(BF)
        second = jnp.dot(hgr_own, both[:, cols], preferred_element_type=F32)
        for j in range(4):
            rows = [second[(i * 4 + j) * 8 : (i * 4 + j) * 8 + 8] for i in range(4)]
            by_y[j, :, cols] = jnp.concatenate(rows, axis=0).astype(BF)


def table_kernel(meta, hid_t, hgr_t, up, pup, u, v, bias, ids, pids, by_x, by_y, hid, hgr):
    core = meta[0]
    n = up.shape[0]
    hid[...] = hid_t[...].astype(F32).T.astype(BF)
    hgr[...] = hgr_t[...].astype(F32).T.astype(BF)
    at = lax.broadcasted_iota(jnp.int32, (128, n), 0)
    row_x = (at // 32) * 64 + core * 32 + at % 32
    row_y = ((at // 8) % 4) * 64 + core * 32 + (at // 32) * 8 + at % 8
    for pair in range(TABLES // 2):
        cols = slice(EMB + pair * 256, EMB + pair * 256 + 256)
        mixed = jnp.dot(hid[...], u[:, cols], preferred_element_type=F32) + bias[:, cols]
        back = jnp.dot(hgr[...], v[:, cols], preferred_element_type=F32)
        up_float = jnp.concatenate([up[:, cols], pup[:, cols]], axis=0).astype(F32)
        pooled = (up_float * (1.0 + mixed) + back).astype(BF)
        for which in range(2):
            table = 2 * pair + which
            owner = meta[1 + table]
            slot = meta[1 + TABLES + table]
            row = row_y if which else row_x
            counts = []
            for source in (ids, pids):
                eight = source[owner]
                four = jnp.where(slot == 0, eight[:4], eight[4:])
                count = jnp.where(four[0:1] == row, 1.0, 0.0)
                for k in range(1, 4):
                    count = count + jnp.where(four[k : k + 1] == row, 1.0, 0.0)
                counts.append(count.astype(BF))
            total = jnp.dot(
                jnp.concatenate(counts, axis=1),
                pooled[:, which * EMB : (which + 1) * EMB],
                preferred_element_type=F32,
            )
            out = by_y if which else by_x
            for i in range(4):
                out[i, pair] = total[i * 32 : (i + 1) * 32].astype(BF)


def sum4(arrived):
    return arrived.astype(F32).sum(axis=0)


def on_device(cross_input, upstream, v_weight, u_weight, bias, placement, owned_ids):
    samples, width = cross_input.shape
    scale = 1.0 / math.sqrt(samples * 256)
    core = lax.axis_index("c").astype(jnp.int32)
    swap = [(0, 1), (1, 0)]
    vmem = pl.BlockSpec(memory_space=pltpu.VMEM)
    smem = pl.BlockSpec(memory_space=pltpu.SMEM)
    params = pltpu.CompilerParams(vmem_limit_bytes=48 << 20)

    with jax.named_scope("ids"):
        ids = owned_ids.astype(jnp.int16).reshape(8, 32, samples).transpose(1, 0, 2)
        ids = lax.all_to_all(ids, ("y", "z"), 0, 0, tiled=True)
        pids = lax.ppermute(ids, "c", swap)
        ids = ids.astype(jnp.int32)
        pids = pids.astype(jnp.int32)

    same = placement[:, None] == placement[None, :]
    earlier = jnp.arange(TABLES)[None, :] < jnp.arange(TABLES)[:, None]
    slot = jnp.sum((same & earlier).astype(jnp.int32), axis=1)
    meta = jnp.concatenate([core[None], placement, slot])

    with jax.named_scope("swap"):
        px = lax.ppermute(cross_input, "c", swap)
        pup = lax.ppermute(upstream, "c", swap)

    hid_t, hgr_t, cross_x, cross_y = pl.pallas_call(
        dense_kernel,
        out_shape=(
            jax.ShapeDtypeStruct((RANK, 2 * samples), BF),
            jax.ShapeDtypeStruct((RANK, 2 * samples), BF),
            jax.ShapeDtypeStruct((4, 32, width), BF),
            jax.ShapeDtypeStruct((4, 32, width), BF),
        ),
        in_specs=[smem] + [vmem] * 6,
        out_specs=(vmem,) * 4,
        scratch_shapes=[
            pltpu.VMEM((2 * samples, width), BF),
            pltpu.VMEM((2 * samples, width), BF),
        ],
        compiler_params=params,
        name="dense",
    )(meta, cross_input, px, upstream, pup, v_weight, u_weight)

    with jax.named_scope("cross1"):
        cross_x = lax.all_to_all(cross_x, "x", 0, 0, tiled=True)
        cross_y = lax.all_to_all(cross_y, "y", 0, 0, tiled=True)

    table_x, table_y = pl.pallas_call(
        table_kernel,
        out_shape=(
            jax.ShapeDtypeStruct((4, TABLES // 2, 32, EMB), BF),
            jax.ShapeDtypeStruct((4, TABLES // 2, 32, EMB), BF),
        ),
        in_specs=[smem] + [vmem] * 9,
        out_specs=(vmem,) * 2,
        scratch_shapes=[
            pltpu.VMEM((2 * samples, RANK), BF),
            pltpu.VMEM((2 * samples, RANK), BF),
        ],
        compiler_params=params,
        name="tables",
    )(meta, hid_t, hgr_t, upstream, pup, u_weight, v_weight, bias[None], ids, pids)

    with jax.named_scope("table1"):
        table_x = lax.all_to_all(table_x, "x", 0, 0, tiled=True)
        table_y = lax.all_to_all(table_y, "y", 0, 0, tiled=True)

    with jax.named_scope("cross2"):
        cross_x = sum4(cross_x).astype(BF).reshape(4, 8, width)
        cross_y = sum4(cross_y).astype(BF).reshape(4, 8, width)
        cross_x = lax.all_to_all(cross_x, "y", 0, 0, tiled=True)
        cross_y = lax.all_to_all(cross_y, "x", 0, 0, tiled=True)

    with jax.named_scope("table2"):
        table_x = sum4(table_x).astype(BF).reshape(TABLES // 2, 4, 8, EMB).transpose(1, 0, 2, 3)
        table_y = sum4(table_y).astype(BF).reshape(TABLES // 2, 4, 8, EMB).transpose(1, 0, 2, 3)
        table_x = lax.all_to_all(table_x, "y", 0, 0, tiled=True)
        table_y = lax.all_to_all(table_y, "x", 0, 0, tiled=True)

    with jax.named_scope("cross3"):
        cross = jnp.concatenate([sum4(cross_x), sum4(cross_y)], axis=1)
        cross = cross.reshape(8, 54, EMB)
        cross = lax.all_to_all(cross, "z", 0, 0, tiled=True)
        cross_grad = (cross.sum(axis=0) * scale).reshape(1, 2 * width)

    with jax.named_scope("table3"):
        tables = jnp.stack([sum4(table_x), sum4(table_y)], axis=1).reshape(TABLES, 8 * EMB)
        place = (placement % 8) * 8 + (placement // 8) * 2 + slot
        select = (jnp.arange(64, dtype=jnp.int32)[:, None] == place[None, :]).astype(BF)
        routed = jnp.dot(select, tables.astype(BF), preferred_element_type=F32).astype(BF)
        routed = routed.reshape(8, 8, 8, EMB)
        routed = lax.all_to_all(routed, "z", 0, 0, tiled=True)
        routed = routed.astype(F32).sum(axis=0).reshape(4, 2, 8, EMB)

    with jax.named_scope("table4"):
        routed = lax.all_to_all(routed, "y", 0, 0, tiled=True)
        table_grad = routed.transpose(1, 0, 2, 3).reshape(2, 32, EMB)
    return (cross_grad, table_grad)


def solution(mesh):
    fine = Mesh(mesh.devices.reshape(4, 2, 4, 8), ("x", "c", "y", "z"))
    grp, tbl = ("x", "c"), ("y", "z")
    in_specs = (
        P(grp + tbl, None),
        P(grp + tbl, None),
        P(),
        P(),
        P(),
        P(),
        P(tbl, None, grp),
    )
    out_specs = (P(grp + tbl, None), P(tbl, grp, None))
    return jax.shard_map(
        on_device, mesh=fine, in_specs=in_specs, out_specs=out_specs, check_vma=False
    )
```

```python
import math

import jax
import jax.numpy as jnp
from jax import lax
from jax.experimental import pallas as pl
from jax.experimental.pallas import tpu as pltpu
from jax.sharding import Mesh
from jax.sharding import PartitionSpec as P

EMB = 128
TABLES = 26
PAIRS = TABLES // 2
RANK = 256
NX, NY, NZ = 4, 4, 8
BF = jnp.bfloat16
F32 = jnp.float32
I32 = jnp.int32
I16 = jnp.int16

X, C, Y, Z, OWNER, SLOT, TABLE_AT = 0, 1, 2, 3, 4, 4 + TABLES, 4 + 2 * TABLES


def nt(left, right):
    return lax.dot_general(left, right, (((1,), (1,)), ((), ())), preferred_element_type=F32)


def mm(left, right):
    return jnp.dot(left, right, preferred_element_type=F32)


def call(kernel, name, outs, meta, *args, scratch=(), flops=0, size=0):
    vmem = pl.BlockSpec(memory_space=pltpu.VMEM)
    smem = pl.BlockSpec(memory_space=pltpu.SMEM)
    return pl.pallas_call(
        kernel,
        out_shape=tuple(jax.ShapeDtypeStruct(shape, dtype) for shape, dtype in outs),
        in_specs=[smem] + [vmem] * len(args),
        out_specs=(vmem,) * len(outs),
        scratch_shapes=[pltpu.VMEM(shape, dtype) for shape, dtype in scratch],
        compiler_params=pltpu.CompilerParams(vmem_limit_bytes=40 << 20),
        cost_estimate=pl.CostEstimate(flops=flops, bytes_accessed=size, transcendentals=0),
        name=name,
    )(meta, *args)


def shift(chunks, axis):
    n = len(chunks)
    return [chunks[0]] + [
        lax.ppermute(chunks[d], axis, [(i, (i + d) % n) for i in range(n)]) for d in range(1, n)
    ]


def ids_to_y(meta, ids, pids, *outs):
    for d in range(NY):
        start = lax.rem(meta[Y] + d, NY) * (NZ * EMB)
        both = [ref[s, :, pl.ds(pl.multiple_of(start, EMB), NZ * EMB)] for ref in (ids, pids) for s in range(2)]
        rows = jnp.concatenate(both, axis=0).astype(I16)
        for z in range(NZ):
            outs[d][z] = rows[:, z * EMB : (z + 1) * EMB]


def ids_to_z(meta, *refs):
    ins, outs = refs[:NY], refs[NY:]
    for d in range(NZ):
        to = lax.rem(meta[Z] + d, NZ)
        for back in range(NY):
            outs[d][back] = ins[back][to]


def dense_kernel(meta, x, px, up, pup, v, u, hid, hgr, *refs):
    outs, (both, prod) = refs[:8], refs[8:]
    n = x.shape[0]
    both[:n] = x[...]
    both[n:] = px[...]
    prod[:n] = (x[...].astype(F32) * up[...].astype(F32)).astype(BF)
    prod[n:] = (px[...].astype(F32) * pup[...].astype(F32)).astype(BF)
    hid_t = nt(v[...], both[...]).astype(BF)
    hgr_t = nt(u[...], prod[...]).astype(BF)
    hid[...] = hid_t.astype(F32).T.astype(BF)
    hgr[...] = hgr_t.astype(F32).T.astype(BF)
    at = lax.broadcasted_iota(I32, (RANK // 2, RANK), 0)
    row = lax.broadcasted_iota(I32, (RANK // 2, RANK), 1)
    to_z = lax.rem(meta[Z] + at % 8, NZ) + meta[C] * 32
    by_x = lax.rem(meta[X] + at // 32, NX) * 64 + lax.rem(meta[Y] + (at // 8) % 4, NY) * 8 + to_z
    by_y = lax.rem(meta[X] + (at // 8) % 4, NX) * 64 + lax.rem(meta[Y] + at // 32, NY) * 8 + to_z
    hid_own = mm((row == by_x).astype(F32).astype(BF), hid_t).astype(BF)
    hgr_own = mm((row == by_y).astype(F32).astype(BF), hgr_t).astype(BF)
    width = 1152
    for k in range(x.shape[1] // width):
        cols = slice(k * width, (k + 1) * width)
        first = mm(hid_own, prod[:, cols])
        second = mm(hgr_own, both[:, cols])
        for d in range(4):
            outs[d][:, cols] = first[d * 32 : (d + 1) * 32].astype(outs[d].dtype)
            outs[4 + d][:, cols] = second[d * 32 : (d + 1) * 32].astype(outs[4 + d].dtype)


def table_kernel(meta, hid, hgr, up, pup, u, v, bias, *refs):
    msgs, outs, ids = refs[:8], refs[8:16], refs[16]
    n = up.shape[0]
    for d in range(NZ):
        ids[d] = msgs[d][...].astype(I32)
    at = lax.broadcasted_iota(I32, (RANK // 2, n), 0)
    row_x = lax.rem(meta[X] + at // 32, NX) * 64 + lax.rem(meta[Y] + (at // 8) % 4, NY) * 8
    row_y = lax.rem(meta[X] + (at // 8) % 4, NX) * 64 + lax.rem(meta[Y] + at // 32, NY) * 8
    row_x = row_x + at % 8 + meta[C] * 32
    row_y = row_y + at % 8 + meta[C] * 32
    for pair in range(PAIRS):
        cols = slice(EMB + pair * 256, EMB + pair * 256 + 256)
        mixed = mm(hid[...], u[:, cols]) + bias[:, cols]
        back = mm(hgr[...], v[:, cols])
        up_float = jnp.concatenate([up[:, cols], pup[:, cols]], axis=0).astype(F32)
        pooled = (up_float * (1.0 + mixed) + back).astype(BF)
        for which in range(2):
            table = 2 * pair + which
            owner = meta[OWNER + table]
            slot = meta[SLOT + table]
            from_y = lax.rem(meta[Y] - owner // NZ + NY, NY)
            from_z = lax.rem(meta[Z] - owner % NZ + NZ, NZ)
            looked = ids[from_z, from_y]
            row = row_y if which else row_x
            counts = []
            for half in range(2):
                eight = looked[half * 8 : half * 8 + 8]
                four = jnp.where(slot == 0, eight[:4], eight[4:])
                count = jnp.where(four[0:1] == row, 1.0, 0.0)
                for k in range(1, 4):
                    count = count + jnp.where(four[k : k + 1] == row, 1.0, 0.0)
                counts.append(count.astype(BF))
            total = mm(
                jnp.concatenate(counts, axis=1), pooled[:, which * EMB : (which + 1) * EMB]
            )
            for d in range(4):
                out = outs[4 * which + d]
                out[pair] = total[d * 32 : (d + 1) * 32].astype(out.dtype)


def total_of(refs):
    total = refs[0][...].astype(F32)
    for ref in refs[1:]:
        total = total + ref[...].astype(F32)
    return total


def cross_second(meta, *refs):
    for side in range(2):
        total = total_of(refs[4 * side : 4 * side + 4])
        outs = refs[8 + 4 * side : 12 + 4 * side]
        for d in range(4):
            outs[d][...] = total[d * 8 : (d + 1) * 8].astype(outs[d].dtype)


def table_second(meta, *refs):
    for side in range(2):
        total = total_of(refs[4 * side : 4 * side + 4])
        outs = refs[8 + 4 * side : 12 + 4 * side]
        for d in range(4):
            outs[d][...] = total[:, d * 8 : (d + 1) * 8].astype(outs[d].dtype)


def to_z_kernel(meta, *refs):
    cross, tables, outs, (sums, held) = refs[:8], refs[8:16], refs[16:24], refs[24:]
    width = cross[0].shape[1]
    blocks = width // EMB
    for side in range(2):
        total = total_of(cross[4 * side : 4 * side + 4])
        for k in range(blocks):
            sums[:, side * blocks + k] = total[:, k * EMB : (k + 1) * EMB]
    held[0] = jnp.zeros((8, EMB), F32)
    for side in range(2):
        total = total_of(tables[4 * side : 4 * side + 4])
        for pair in range(PAIRS):
            held[1 + 2 * pair + side] = total[pair]
    for d in range(NZ):
        z = lax.rem(meta[Z] + d, NZ)
        slots = []
        for e in range(NY):
            device = lax.rem(meta[Y] + e, NY) * NZ + z
            for s in range(2):
                slots.append(held[meta[TABLE_AT + 2 * device + s]])
        outs[d][:64] = jnp.concatenate(slots, axis=0).astype(outs[d].dtype)
        outs[d][64:] = sums[d].astype(outs[d].dtype)


def to_y_kernel(meta, *refs):
    msgs, cross, outs = refs[:8], refs[8], refs[9:]
    total = total_of(msgs)
    blocks = cross.shape[1] // EMB
    scale = 1.0 / math.sqrt(EMB * 256)
    for k in range(blocks):
        cross[:, k * EMB : (k + 1) * EMB] = total[64 + k : 65 + k] * scale
    for e in range(NY):
        outs[e][...] = total[e * 16 : (e + 1) * 16]


def place_kernel(meta, *refs):
    msgs, out = refs[:4], refs[4]
    for e in range(NY):
        start = pl.multiple_of(lax.rem(meta[Y] + NY - e, NY) * 8, 8)
        for s in range(2):
            out[s, pl.ds(start, 8)] = msgs[e][s * 8 : (s + 1) * 8]


def on_device(cross_input, upstream, v_weight, u_weight, bias, placement, owned_ids):
    samples, width = cross_input.shape
    swap = [(0, 1), (1, 0)]
    pids = lax.ppermute(owned_ids, "c", swap)
    px = lax.ppermute(cross_input, "c", swap)
    pup = lax.ppermute(upstream, "c", swap)

    same = placement[:, None] == placement[None, :]
    earlier = jnp.arange(TABLES)[None, :] < jnp.arange(TABLES)[:, None]
    slot = jnp.sum((same & earlier).astype(I32), axis=1)
    target = placement * 2 + slot
    table_at = jnp.sum(
        jnp.where(
            jnp.arange(64, dtype=I32)[:, None] == target[None, :],
            jnp.arange(1, TABLES + 1, dtype=I32)[None, :],
            0,
        ),
        axis=1,
    )
    position = jnp.stack([lax.axis_index(axis).astype(I32) for axis in ("x", "c", "y", "z")])
    meta = jnp.concatenate([position, placement, slot, table_at])

    ids = call(ids_to_y, "ids_to_y", [((NZ, 16, EMB), I16)] * NY, meta, owned_ids, pids, size=400000)
    ids = shift(ids, "y")
    ids = call(ids_to_z, "ids_to_z", [((NY, 16, EMB), I16)] * NZ, meta, *ids, size=260000)
    ids = shift(ids, "z")

    def own_and_sent(shape):
        return [(shape, F32)] + [(shape, BF)] * 3

    hid, hgr, *cross = call(
        dense_kernel,
        "dense",
        [((2 * samples, RANK), BF)] * 2 + own_and_sent((32, width)) * 2,
        meta,
        cross_input,
        px,
        upstream,
        pup,
        v_weight,
        u_weight,
        scratch=[((2 * samples, width), BF)] * 2,
        flops=6 * 256 * 256 * width,
        size=9 << 20,
    )
    cross = shift(cross[:4], "x") + shift(cross[4:], "y")

    tables = call(
        table_kernel,
        "tables",
        own_and_sent((PAIRS, 32, EMB)) * 2,
        meta,
        hid,
        hgr,
        upstream,
        pup,
        u_weight,
        v_weight,
        bias[None],
        *ids,
        scratch=[((NZ, NY, 16, EMB), I32)],
        flops=6 * 256 * 256 * width,
        size=9 << 20,
    )
    tables = shift(tables[:4], "x") + shift(tables[4:], "y")

    cross = call(cross_second, "cross_second", own_and_sent((8, width)) * 2, meta, *cross, size=3 << 20)
    cross = shift(cross[:4], "y") + shift(cross[4:], "x")
    tables = call(table_second, "table_second", own_and_sent((PAIRS, 8, EMB)) * 2, meta, *tables, size=1 << 20)
    tables = shift(tables[:4], "y") + shift(tables[4:], "x")

    rows = 64 + 2 * width // EMB
    msgs = call(
        to_z_kernel,
        "to_z",
        [((rows, EMB), F32)] + [((rows, EMB), BF)] * (NZ - 1),
        meta,
        *cross,
        *tables,
        scratch=[((8, 2 * width // EMB, EMB), F32), ((TABLES + 1, 8, EMB), F32)],
        size=1 << 20,
    )
    msgs = shift(msgs, "z")
    cross_grad, *routed = call(
        to_y_kernel, "to_y", [((1, 2 * width), F32)] + [((16, EMB), F32)] * NY, meta, *msgs, size=400000
    )
    routed = shift(routed, "y")
    (table_grad,) = call(place_kernel, "place", [((2, 32, EMB), F32)], meta, *routed, size=64000)
    return (cross_grad, table_grad)


def solution(mesh):
    fine = Mesh(mesh.devices.reshape(NX, 2, NY, NZ), ("x", "c", "y", "z"))
    grp, tbl = ("x", "c"), ("y", "z")
    in_specs = (
        P(grp + tbl, None),
        P(grp + tbl, None),
        P(),
        P(),
        P(),
        P(),
        P(tbl, None, grp),
    )
    out_specs = (P(grp + tbl, None), P(tbl, grp, None))
    return jax.shard_map(
        on_device, mesh=fine, in_specs=in_specs, out_specs=out_specs, check_vma=False
    )
```

```python
import math

import jax
import jax.numpy as jnp
from jax import lax
from jax.experimental import pallas as pl
from jax.experimental.pallas import tpu as pltpu
from jax.sharding import Mesh
from jax.sharding import PartitionSpec as P

EMB = 128
TABLES = 26
RANK = 256
NX, NY, NZ = 4, 4, 8
NJ = NY * NZ
BF = jnp.bfloat16
F32 = jnp.float32
I32 = jnp.int32
I16 = jnp.int16

CORE, ME, OWNER, SLOT, TABLE_AT = 0, 1, 2, 2 + TABLES, 2 + 2 * TABLES
VMEM = pl.BlockSpec(memory_space=pltpu.VMEM)
SMEM = pl.BlockSpec(memory_space=pltpu.SMEM)
HBM = pl.BlockSpec(memory_space=pltpu.HBM)


def nt(left, right):
    return lax.dot_general(left, right, (((1,), (1,)), ((), ())), preferred_element_type=F32)


def mm(left, right):
    return jnp.dot(left, right, preferred_element_type=F32)


def call(kernel, name, outs, *args, specs=None, out_specs=None, scratch=(), flops=0, size=0, vmem=24 << 20):
    return pl.pallas_call(
        kernel,
        out_shape=tuple(jax.ShapeDtypeStruct(shape, dtype) for shape, dtype in outs),
        in_specs=specs or [SMEM] + [VMEM] * (len(args) - 1),
        out_specs=tuple(out_specs or [VMEM] * len(outs)),
        scratch_shapes=list(scratch),
        compiler_params=pltpu.CompilerParams(vmem_limit_bytes=vmem),
        cost_estimate=pl.CostEstimate(flops=flops, bytes_accessed=size, transcendentals=0),
        name=name,
    )(*args)


def half_of(bit):
    return [p for p in range(NJ) if p >> bit & 1]


def ids_start(meta, ids, pids, state, sent, *, bit):
    for p in range(NJ):
        start = pl.multiple_of(jnp.bitwise_xor(meta[ME], p) * EMB, EMB)
        parts = [ref[s, :, pl.ds(start, EMB)] for ref in (ids, pids) for s in range(2)]
        state[p] = jnp.concatenate(parts, axis=0).astype(I16)
    for k, p in enumerate(half_of(bit)):
        sent[k] = state[p]


def ids_step(old, came, state, sent, *, last, bit):
    for p in range(NJ):
        if not p >> last & 1:
            state[p] = old[p]
    for k, p in enumerate(half_of(last)):
        state[p] = came[k]
    for k, p in enumerate(half_of(bit)):
        sent[k] = state[p]


def own_rows(full, core):
    picks = [
        jnp.where(core == 0, full[i * 64 : i * 64 + 32], full[i * 64 + 32 : i * 64 + 64])
        for i in range(NX)
    ]
    return jnp.concatenate(picks, axis=0)


def loads_of(pairs, sems):
    loads = [
        pltpu.make_async_copy(source, target, sems.at[k])
        for k, (source, target) in enumerate(pairs)
    ]
    for load in loads:
        load.start()
    return loads


def dense_kernel(meta, x, px, up, pup, v, u, hid_out, hgr_out, out, *scratch):
    both, ups, vv, uu, prod, hid, hgr, held, in_sems, out_sems = scratch
    n, width = x.shape
    loads = loads_of(
        (
            (x, both.at[:n]),
            (px, both.at[n:]),
            (v, vv),
            (up, ups.at[:n]),
            (pup, ups.at[n:]),
            (u, uu),
        ),
        in_sems,
    )
    for load in loads[:3]:
        load.wait()
    hid[...] = nt(vv[...], both[...]).astype(BF)
    loads[3].wait()
    loads[4].wait()
    prod[...] = (both[...].astype(F32) * ups[...].astype(F32)).astype(BF)
    loads[5].wait()
    hgr[...] = nt(uu[...], prod[...]).astype(BF)
    copies = loads_of(((hid, hid_out), (hgr, hgr_out)), out_sems)
    hid_own = own_rows(hid[...].astype(F32), meta[CORE]).astype(BF)
    hgr_own = own_rows(hgr[...].astype(F32), meta[CORE]).astype(BF)
    step = 1152
    for side, (left, right) in enumerate(((hid_own, prod), (hgr_own, both))):
        for k in range(width // step):
            total = mm(left, right[:, k * step : (k + 1) * step])
            cols = slice(side * width + k * step, side * width + (k + 1) * step)
            for i in range(NX):
                held[i, :, cols] = total[i * 32 : (i + 1) * 32].astype(BF)
            copies.append(
                pltpu.make_async_copy(
                    held.at[:, :, cols], out.at[:, :, cols], out_sems.at[len(copies)]
                )
            )
            copies[-1].start()
    for copy in copies:
        copy.wait()


def table_kernel(meta, hid_in, hgr_in, up_in, pup_in, u_in, v_in, bias, ids, came, out, *scratch, last):
    state, counts, hid, hgr, ups, u, v, held, in_sems, out_sem = scratch
    n = up_in.shape[0]
    loads = loads_of(
        (
            (hid_in, hid),
            (hgr_in, hgr),
            (u_in, u),
            (v_in, v),
            (up_in, ups.at[:n]),
            (pup_in, ups.at[n:]),
        ),
        in_sems,
    )
    for p in range(NJ):
        if not p >> last & 1:
            state[p] = ids[p].astype(I32)
    for k, p in enumerate(half_of(last)):
        state[p] = came[k].astype(I32)
    at = lax.broadcasted_iota(I32, (RANK // 2, n), 0)
    row = (at // 32) * 64 + meta[CORE] * 32 + at % 32
    for table in range(TABLES):
        slot = meta[SLOT + table]
        looked = state[jnp.bitwise_xor(meta[ME], meta[OWNER + table])]
        for half in range(2):
            eight = looked[half * 8 : half * 8 + 8]
            four = jnp.where(slot == 0, eight[:4], eight[4:])
            count = jnp.where(four[0:1] == row, 1.0, 0.0)
            for k in range(1, 4):
                count = count + jnp.where(four[k : k + 1] == row, 1.0, 0.0)
            counts[table, :, half * n : (half + 1) * n] = count.astype(BF)
    for load in loads:
        load.wait()
    hid_s = hid[...].astype(F32).T.astype(BF)
    hgr_s = hgr[...].astype(F32).T.astype(BF)
    for pair in range(TABLES // 2):
        cols = slice(EMB + pair * 256, EMB + pair * 256 + 256)
        mixed = mm(hid_s, u[:, cols]) + bias[:, cols]
        back = mm(hgr_s, v[:, cols])
        pooled = (ups[:, cols].astype(F32) * (1.0 + mixed) + back).astype(BF)
        for which in range(2):
            table = 2 * pair + which
            total = mm(counts[table], pooled[:, which * EMB : (which + 1) * EMB])
            for k in range(NX * NY):
                held[k, table] = total[k * 8 : (k + 1) * 8].astype(BF)
    copy = pltpu.make_async_copy(held, out, out_sem.at[0])
    copy.start()
    copy.wait()


def cross_kernel(came, out, sums):
    blocks = came.shape[2] // EMB
    for k in range(blocks):
        cols = slice(k * EMB, (k + 1) * EMB)
        total = came[0, :, cols].astype(F32)
        for i in range(1, NX):
            total = total + came[i, :, cols].astype(F32)
        sums[:, k] = total
    for j in range(NJ):
        out[j] = sums[j].astype(BF)


def route_kernel(meta, came, cross, out, held):
    held[0] = jnp.zeros((8, EMB), F32)
    total = came[0].astype(F32)
    for k in range(1, NX * NY):
        total = total + came[k].astype(F32)
    held[1:] = total
    for j in range(NJ):
        slots = [held[meta[TABLE_AT + 2 * j + s]] for s in range(2)]
        out[j, :16] = jnp.concatenate(slots, axis=0).astype(BF)
        out[j, 16:] = cross[j]


def last_kernel(came, cross, table):
    blocks = cross.shape[1] // EMB
    scale = 1.0 / math.sqrt(EMB * 256)
    total = came[0, 16:].astype(F32)
    for j in range(1, NJ):
        total = total + came[j, 16:].astype(F32)
    for k in range(blocks):
        cross[:, k * EMB : (k + 1) * EMB] = total[k : k + 1] * scale
    for y in range(NY):
        rows = came[y * NZ, :16].astype(F32)
        for z in range(1, NZ):
            rows = rows + came[y * NZ + z, :16].astype(F32)
        for s in range(2):
            table[s, y * 8 : (y + 1) * 8] = rows[s * 8 : (s + 1) * 8]


def on_device(cross_input, upstream, v_weight, u_weight, bias, placement, owned_ids):
    samples, width = cross_input.shape
    swap = [(0, 1), (1, 0)]
    pids = lax.ppermute(owned_ids, "c", swap)
    px = lax.ppermute(cross_input, "c", swap)
    pup = lax.ppermute(upstream, "c", swap)

    same = placement[:, None] == placement[None, :]
    earlier = jnp.arange(TABLES)[None, :] < jnp.arange(TABLES)[:, None]
    slot = jnp.sum((same & earlier).astype(I32), axis=1)
    target = placement * 2 + slot
    table_at = jnp.sum(
        jnp.where(
            jnp.arange(2 * NJ, dtype=I32)[:, None] == target[None, :],
            jnp.arange(1, TABLES + 1, dtype=I32)[None, :],
            0,
        ),
        axis=1,
    )
    position = jnp.stack([lax.axis_index("c"), lax.axis_index(("y", "z"))]).astype(I32)
    meta = jnp.concatenate([position, placement, slot, table_at])

    bits = [4, 3, 2, 1, 0]
    pieces = [((NJ, 16, EMB), I16), ((NJ // 2, 16, EMB), I16)]

    def swap_bit(sent, bit):
        return lax.ppermute(sent, ("y", "z"), [(j, j ^ 1 << bit) for j in range(NJ)])

    def start(*refs):
        ids_start(*refs, bit=bits[0])

    state, sent = call(start, "ids_start", pieces, meta, owned_ids, pids, size=400000)
    came = swap_bit(sent, bits[0])
    px, came = lax.optimization_barrier((px, came))
    for last, bit in zip(bits[:-1], bits[1:]):

        def step(*refs, last=last, bit=bit):
            ids_step(*refs, last=last, bit=bit)

        state, sent = call(
            step, f"ids_bit{bit}", pieces, state, came, specs=[VMEM] * 2, size=400000
        )
        came = swap_bit(sent, bit)

    hid2, hgr2, cross = call(
        dense_kernel,
        "dense",
        [((RANK, 2 * samples), BF)] * 2 + [((NX, NJ, 2 * width), BF)],
        meta,
        cross_input,
        px,
        upstream,
        pup,
        v_weight,
        u_weight,
        specs=[SMEM] + [HBM] * 6,
        out_specs=[HBM] * 3,
        scratch=[pltpu.VMEM((256, width), BF)] * 5
        + [pltpu.VMEM((RANK, 2 * samples), BF)] * 2
        + [
            pltpu.VMEM((NX, NJ, 2 * width), BF),
            pltpu.SemaphoreType.DMA((6,)),
            pltpu.SemaphoreType.DMA((8,)),
        ],
        vmem=56 << 20,
        flops=6 * 256 * 256 * width,
        size=6 << 20,
    )
    cross = lax.all_to_all(cross, "x", 0, 0, tiled=True)

    def tables_of(*refs):
        table_kernel(*refs, last=bits[-1])

    (tables,) = call(
        tables_of,
        "tables",
        [((NX * NY, TABLES, 8, EMB), BF)],
        meta,
        hid2,
        hgr2,
        upstream,
        pup,
        u_weight,
        v_weight,
        bias[None],
        state,
        came,
        specs=[SMEM] + [HBM] * 6 + [VMEM] * 3,
        out_specs=[HBM],
        scratch=[
            pltpu.VMEM((NJ, 16, EMB), I32),
            pltpu.VMEM((TABLES, RANK // 2, 2 * samples), BF),
        ]
        + [pltpu.VMEM((RANK, 2 * samples), BF)] * 2
        + [pltpu.VMEM((256, width), BF)] * 3
        + [
            pltpu.VMEM((NX * NY, TABLES, 8, EMB), BF),
            pltpu.SemaphoreType.DMA((6,)),
            pltpu.SemaphoreType.DMA((1,)),
        ],
        vmem=56 << 20,
        flops=6 * 256 * 256 * width,
        size=9 << 20,
    )
    tables = lax.all_to_all(tables, ("x", "y"), 0, 0, tiled=True)

    blocks = 2 * width // EMB
    (cross,) = call(
        cross_kernel,
        "cross_sum",
        [((NJ, blocks, EMB), BF)],
        cross,
        specs=[VMEM],
        scratch=[pltpu.VMEM((NJ, blocks, EMB), F32)],
        size=3 << 20,
    )
    (routed,) = call(
        route_kernel,
        "route",
        [((NJ, 16 + blocks, EMB), BF)],
        meta,
        tables,
        cross,
        scratch=[pltpu.VMEM((TABLES + 1, 8, EMB), F32)],
        size=3 << 20,
    )
    routed = lax.all_to_all(routed, ("y", "z"), 0, 0, tiled=True)
    return call(
        last_kernel,
        "last",
        [((1, 2 * width), F32), ((2, NJ, EMB), F32)],
        routed,
        specs=[VMEM],
        size=1 << 20,
    )


def solution(mesh):
    fine = Mesh(mesh.devices.reshape(NX, 2, NY, NZ), ("x", "c", "y", "z"))
    grp, tbl = ("x", "c"), ("y", "z")
    in_specs = (
        P(grp + tbl, None),
        P(grp + tbl, None),
        P(),
        P(),
        P(),
        P(),
        P(tbl, None, grp),
    )
    out_specs = (P(grp + tbl, None), P(tbl, grp, None))
    return jax.shard_map(
        on_device, mesh=fine, in_specs=in_specs, out_specs=out_specs, check_vma=False
    )
```

```python
import math

import jax
import jax.numpy as jnp
from jax import lax
from jax.experimental import pallas as pl
from jax.experimental.pallas import tpu as pltpu
from jax.sharding import Mesh
from jax.sharding import PartitionSpec as P

EMB = 128
TABLES = 26
RANK = 256
NX, NY, NZ = 4, 4, 8
NJ = NY * NZ
BF = jnp.bfloat16
F32 = jnp.float32
I32 = jnp.int32
I16 = jnp.int16

CORE, XX, YY, OWNER, SLOT, TABLE_AT = 0, 1, 2, 3, 3 + TABLES, 3 + 2 * TABLES
VMEM = pl.BlockSpec(memory_space=pltpu.VMEM)
SMEM = pl.BlockSpec(memory_space=pltpu.SMEM)
HBM = pl.BlockSpec(memory_space=pltpu.HBM)


def nt(left, right):
    return lax.dot_general(left, right, (((1,), (1,)), ((), ())), preferred_element_type=F32)


def mm(left, right):
    return jnp.dot(left, right, preferred_element_type=F32)


def call(kernel, name, outs, *args, specs=None, out_specs=None, scratch=(), flops=0, size=0, vmem=24 << 20):
    return pl.pallas_call(
        kernel,
        out_shape=tuple(jax.ShapeDtypeStruct(shape, dtype) for shape, dtype in outs),
        in_specs=specs or [SMEM] + [VMEM] * (len(args) - 1),
        out_specs=tuple(out_specs or [VMEM] * len(outs)),
        scratch_shapes=list(scratch),
        compiler_params=pltpu.CompilerParams(vmem_limit_bytes=vmem),
        cost_estimate=pl.CostEstimate(flops=flops, bytes_accessed=size, transcendentals=0),
        name=name,
    )(*args)


def ids_kernel(ids, out):
    for j in range(NJ):
        parts = [ids[s, :, j * EMB : (j + 1) * EMB] for s in range(2)]
        out[j] = jnp.concatenate(parts, axis=0).astype(I16)


def own_rows(full, core):
    picks = [
        jnp.where(core == 0, full[i * 64 : i * 64 + 32], full[i * 64 + 32 : i * 64 + 64])
        for i in range(NX)
    ]
    return jnp.concatenate(picks, axis=0)


def loads_of(pairs, sems):
    loads = [
        pltpu.make_async_copy(source, target, sems.at[k])
        for k, (source, target) in enumerate(pairs)
    ]
    for load in loads:
        load.start()
    return loads


def dense_kernel(meta, x, px, up, pup, v, u, hid_out, hgr_out, out, *scratch):
    both, ups, vv, uu, prod, hid, hgr, held, in_sems, out_sems = scratch
    n, width = x.shape
    loads = loads_of(((x, both.at[:n]), (v, vv), (up, ups), (u, uu)), in_sems)
    both[n:] = px[...]
    prod[n:] = (px[...].astype(F32) * pup[...].astype(F32)).astype(BF)
    loads[0].wait()
    loads[1].wait()
    hid[...] = nt(vv[...], both[...]).astype(BF)
    loads[2].wait()
    prod[:n] = (both[:n].astype(F32) * ups[...].astype(F32)).astype(BF)
    loads[3].wait()
    hgr[...] = nt(uu[...], prod[...]).astype(BF)
    copies = loads_of(((hid, hid_out), (hgr, hgr_out)), out_sems)
    hid_own = own_rows(hid[...].astype(F32), meta[CORE]).astype(BF)
    hgr_own = own_rows(hgr[...].astype(F32), meta[CORE]).astype(BF)
    step = 1152
    for side, (left, right) in enumerate(((hid_own, prod), (hgr_own, both))):
        for k in range(width // step):
            total = mm(left, right[:, k * step : (k + 1) * step])
            cols = slice(side * width + k * step, side * width + (k + 1) * step)
            for i in range(NX * NY):
                held[i, :, cols] = total[i * 8 : (i + 1) * 8].astype(BF)
            copies.append(
                pltpu.make_async_copy(
                    held.at[:, :, cols], out.at[:, :, cols], out_sems.at[len(copies)]
                )
            )
            copies[-1].start()
    for copy in copies:
        copy.wait()


def table_kernel(meta, hid_in, hgr_in, up_in, u_in, v_in, pup, bias, ids, pids, *refs):
    outs, (state, counts, hid, hgr, up, u, v) = refs[:4], refs[4:11]
    held, in_sems, out_sems = refs[11:15], refs[15], refs[16]
    n = up_in.shape[0]
    loads = loads_of(((hid_in, hid), (hgr_in, hgr), (u_in, u), (v_in, v), (up_in, up)), in_sems)
    for p in range(NJ):
        state[p, :8] = ids[p].astype(I32)
        state[p, 8:] = pids[p].astype(I32)
    at = lax.broadcasted_iota(I32, (RANK // 2, n), 0)
    row = lax.rem(meta[XX] + (at // 8) % 4, NX) * 64 + lax.rem(meta[YY] + at // 32, NY) * 8
    row = row + meta[CORE] * 32 + at % 8
    for table in range(TABLES):
        slot = meta[SLOT + table]
        looked = state[meta[OWNER + table]]
        for half in range(2):
            eight = looked[half * 8 : half * 8 + 8]
            four = jnp.where(slot == 0, eight[:4], eight[4:])
            count = jnp.where(four[0:1] == row, 1.0, 0.0)
            for k in range(1, 4):
                count = count + jnp.where(four[k : k + 1] == row, 1.0, 0.0)
            counts[table, :, half * n : (half + 1) * n] = count.astype(BF)
    for load in loads:
        load.wait()
    hid_s = hid[...].astype(F32).T.astype(BF)
    hgr_s = hgr[...].astype(F32).T.astype(BF)
    for pair in range(TABLES // 2):
        cols = slice(EMB + pair * 256, EMB + pair * 256 + 256)
        mixed = mm(hid_s, u[:, cols]) + bias[:, cols]
        back = mm(hgr_s, v[:, cols])
        up_float = jnp.concatenate([up[:, cols], pup[:, cols]], axis=0).astype(F32)
        pooled = (up_float * (1.0 + mixed) + back).astype(BF)
        for which in range(2):
            table = 2 * pair + which
            total = mm(counts[table], pooled[:, which * EMB : (which + 1) * EMB])
            for d in range(NY):
                held[d][table] = total[d * 32 : (d + 1) * 32].astype(held[d].dtype)
    for copy in loads_of(tuple(zip(held, outs)), out_sems):
        copy.wait()


def total_of(refs):
    total = refs[0][...].astype(F32)
    for ref in refs[1:]:
        total = total + ref[...].astype(F32)
    return total


def table_second(*refs):
    total = total_of(refs[:NY])
    for d in range(NX):
        refs[NY + d][...] = total[:, d * 8 : (d + 1) * 8].astype(refs[NY + d].dtype)


def cross_kernel(came, out, sums):
    for k in range(came.shape[2] // EMB):
        cols = slice(k * EMB, (k + 1) * EMB)
        total = came[0, :, cols].astype(F32)
        for i in range(1, NX * NY):
            total = total + came[i, :, cols].astype(F32)
        sums[:, k] = total
    out[...] = sums[...].astype(BF)


def cross_last(came, out):
    scale = 1.0 / math.sqrt(EMB * 256)
    total = came[0].astype(F32)
    for z in range(1, NZ):
        total = total + came[z].astype(F32)
    for k in range(total.shape[0]):
        out[:, k * EMB : (k + 1) * EMB] = total[k : k + 1] * scale


def route_kernel(meta, *refs):
    came, out, held = refs[:NX], refs[NX], refs[NX + 1]
    held[0] = jnp.zeros((8, EMB), F32)
    held[1:] = total_of(came)
    for j in range(NJ):
        slots = [held[meta[TABLE_AT + 2 * j + s]] for s in range(2)]
        out[j] = jnp.concatenate(slots, axis=0).astype(BF)


def table_last(came, table):
    for y in range(NY):
        rows = came[y * NZ].astype(F32)
        for z in range(1, NZ):
            rows = rows + came[y * NZ + z].astype(F32)
        for s in range(2):
            table[s, y * 8 : (y + 1) * 8] = rows[s * 8 : (s + 1) * 8]


def shift(chunks, axis):
    n = len(chunks)
    return [chunks[0]] + [
        lax.ppermute(chunks[d], axis, [(i, (i + d) % n) for i in range(n)]) for d in range(1, n)
    ]


def on_device(cross_input, upstream, v_weight, u_weight, bias, placement, owned_ids):
    samples, width = cross_input.shape
    blocks = 2 * width // EMB
    swap = [(0, 1), (1, 0)]
    px = lax.ppermute(cross_input, "c", swap)
    pup = lax.ppermute(upstream, "c", swap)

    (ids,) = call(ids_kernel, "ids", [((NJ, 8, EMB), I16)], owned_ids, specs=[VMEM], size=200000)
    ids = lax.all_to_all(ids, ("y", "z"), 0, 0, tiled=True)

    same = placement[:, None] == placement[None, :]
    earlier = jnp.arange(TABLES)[None, :] < jnp.arange(TABLES)[:, None]
    slot = jnp.sum((same & earlier).astype(I32), axis=1)
    target = placement * 2 + slot
    table_at = jnp.sum(
        jnp.where(
            jnp.arange(2 * NJ, dtype=I32)[:, None] == target[None, :],
            jnp.arange(1, TABLES + 1, dtype=I32)[None, :],
            0,
        ),
        axis=1,
    )
    position = jnp.stack([lax.axis_index(axis) for axis in ("c", "x", "y")]).astype(I32)
    meta = jnp.concatenate([position, placement, slot, table_at])

    wide = pltpu.VMEM((256, width), BF)
    half = pltpu.VMEM((samples, width), BF)
    square = pltpu.VMEM((RANK, 2 * samples), BF)
    hid, hgr, cross = call(
        dense_kernel,
        "dense",
        [((RANK, 2 * samples), BF)] * 2 + [((NX * NY, NZ, 2 * width), BF)],
        meta,
        cross_input,
        px,
        upstream,
        pup,
        v_weight,
        u_weight,
        specs=[SMEM, HBM, VMEM, HBM, VMEM, HBM, HBM],
        out_specs=[HBM] * 3,
        scratch=[wide, half, wide, wide, wide, square, square]
        + [
            pltpu.VMEM((NX * NY, NZ, 2 * width), BF),
            pltpu.SemaphoreType.DMA((4,)),
            pltpu.SemaphoreType.DMA((8,)),
        ],
        vmem=56 << 20,
        flops=6 * 256 * 256 * width,
        size=6 << 20,
    )
    ids, cross = lax.optimization_barrier((ids, cross))
    cross = lax.all_to_all(cross, ("x", "y"), 0, 0, tiled=True)
    pids = lax.ppermute(ids, "c", swap)

    sent = [((TABLES, 32, EMB), F32)] + [((TABLES, 32, EMB), BF)] * 3
    tables = call(
        table_kernel,
        "tables",
        sent,
        meta,
        hid,
        hgr,
        upstream,
        u_weight,
        v_weight,
        pup,
        bias[None],
        ids,
        pids,
        specs=[SMEM] + [HBM] * 5 + [VMEM] * 4,
        out_specs=[HBM] * 4,
        scratch=[
            pltpu.VMEM((NJ, 16, EMB), I32),
            pltpu.VMEM((TABLES, RANK // 2, 2 * samples), BF),
            square,
            square,
            half,
            wide,
            wide,
        ]
        + [pltpu.VMEM(shape, dtype) for shape, dtype in sent]
        + [pltpu.SemaphoreType.DMA((5,)), pltpu.SemaphoreType.DMA((4,))],
        vmem=56 << 20,
        flops=6 * 256 * 256 * width,
        size=9 << 20,
    )
    tables = shift(tables, "y")
    tables = call(
        table_second,
        "table_second",
        [((TABLES, 8, EMB), F32)] + [((TABLES, 8, EMB), BF)] * 3,
        *tables,
        specs=[VMEM] * 4,
        size=1 << 20,
    )
    (cross,) = call(
        cross_kernel,
        "cross_sum",
        [((NZ, blocks, EMB), BF)],
        cross,
        specs=[VMEM],
        scratch=[pltpu.VMEM((NZ, blocks, EMB), F32)],
        size=3 << 20,
    )
    cross = lax.all_to_all(cross, "z", 0, 0, tiled=True)
    tables = shift(tables, "x")
    (routed,) = call(
        route_kernel,
        "route",
        [((NJ, 16, EMB), BF)],
        meta,
        *tables,
        scratch=[pltpu.VMEM((TABLES + 1, 8, EMB), F32)],
        size=1 << 20,
    )
    cross, routed = lax.optimization_barrier((cross, routed))
    routed = lax.all_to_all(routed, ("y", "z"), 0, 0, tiled=True)
    (cross_grad,) = call(
        cross_last, "cross_last", [((1, 2 * width), F32)], cross, specs=[VMEM], size=200000
    )
    (table_grad,) = call(
        table_last, "table_last", [((2, 32, EMB), F32)], routed, specs=[VMEM], size=200000
    )
    return (cross_grad, table_grad)


def solution(mesh):
    fine = Mesh(mesh.devices.reshape(NX, 2, NY, NZ), ("x", "c", "y", "z"))
    grp, tbl = ("x", "c"), ("y", "z")
    in_specs = (
        P(grp + tbl, None),
        P(grp + tbl, None),
        P(),
        P(),
        P(),
        P(),
        P(tbl, None, grp),
    )
    out_specs = (P(grp + tbl, None), P(tbl, grp, None))
    return jax.shard_map(
        on_device, mesh=fine, in_specs=in_specs, out_specs=out_specs, check_vma=False
    )
```

```python
import math

import jax
import jax.numpy as jnp
from jax import lax
from jax.experimental import pallas as pl
from jax.experimental.pallas import tpu as pltpu
from jax.sharding import Mesh
from jax.sharding import PartitionSpec as P

EMB = 128
TABLES = 26
RANK = 256
NX, NY, NZ = 4, 4, 8
NJ = NY * NZ
BF = jnp.bfloat16
F32 = jnp.float32
I32 = jnp.int32
I16 = jnp.int16

VMEM = pl.BlockSpec(memory_space=pltpu.VMEM)
SMEM = pl.BlockSpec(memory_space=pltpu.SMEM)
HBM = pl.BlockSpec(memory_space=pltpu.HBM)


def nt(left, right):
    return lax.dot_general(left, right, (((1,), (1,)), ((), ())), preferred_element_type=F32)


def mm(left, right):
    return jnp.dot(left, right, preferred_element_type=F32)


def call(kernel, name, outs, *args, specs=None, out_specs=None, scratch=(), flops=0, size=0, vmem=24 << 20):
    return pl.pallas_call(
        kernel,
        out_shape=tuple(jax.ShapeDtypeStruct(shape, dtype) for shape, dtype in outs),
        in_specs=specs or [SMEM] + [VMEM] * (len(args) - 1),
        out_specs=tuple(out_specs or [VMEM] * len(outs)),
        scratch_shapes=list(scratch),
        compiler_params=pltpu.CompilerParams(vmem_limit_bytes=vmem),
        cost_estimate=pl.CostEstimate(flops=flops, bytes_accessed=size, transcendentals=0),
        name=name,
    )(*args)


def ids_kernel(ids, out):
    for j in range(NJ):
        parts = [ids[s, :, j * EMB : (j + 1) * EMB] for s in range(2)]
        out[j] = jnp.concatenate(parts, axis=0).astype(I16)


def own_rows(full, core):
    picks = [
        jnp.where(core == 0, full[i * 64 : i * 64 + 32], full[i * 64 + 32 : i * 64 + 64])
        for i in range(NX)
    ]
    return jnp.concatenate(picks, axis=0)


def dense_kernel(x, px, up, pup, v_in, u_in, hid, hgr, out, both, prod, v, u, held, in_sems, sems):
    n, width = x.shape
    core = lax.axis_index("c")
    loads = []
    for source, target in ((v_in, v), (u_in, u)):
        for k in range(2):
            rows = slice(k * 128, (k + 1) * 128)
            loads.append(
                pltpu.make_async_copy(source.at[rows], target.at[rows], in_sems.at[len(loads)])
            )
            loads[-1].start()
    both[:n] = x[...]
    both[n:] = px[...]
    prod[:n] = (x[...].astype(F32) * up[...].astype(F32)).astype(BF)
    prod[n:] = (px[...].astype(F32) * pup[...].astype(F32)).astype(BF)
    loads[0].wait()
    loads[1].wait()
    hid[...] = nt(v[...], both[...]).astype(BF)
    loads[2].wait()
    loads[3].wait()
    hgr[...] = nt(u[...], prod[...]).astype(BF)
    hid_own = own_rows(hid[...].astype(F32), core).astype(BF)
    hgr_own = own_rows(hgr[...].astype(F32), core).astype(BF)
    step = 1152
    copies = []
    for side, (left, right) in enumerate(((hid_own, prod), (hgr_own, both))):
        for k in range(width // step):
            total = mm(left, right[:, k * step : (k + 1) * step])
            cols = slice(side * width + k * step, side * width + (k + 1) * step)
            for i in range(NX * NY):
                held[i, :, cols] = total[i * 8 : (i + 1) * 8].astype(BF)
            copies.append(
                pltpu.make_async_copy(
                    held.at[:, :, cols], out.at[:, :, cols], sems.at[len(copies)]
                )
            )
            copies[-1].start()
    for copy in copies:
        copy.wait()


def slots_of(placement, used, visit):
    for j in range(NJ):
        used[j] = 0
    for table in range(TABLES):
        owner = placement[table]
        slot = used[owner]
        used[owner] = slot + 1
        visit(table, owner, slot)


def table_kernel(placement, hid, hgr, up, u, v, pup, bias, ids, pids, *refs):
    outs, (state, counts, used) = refs[:4], refs[4:]
    n = up.shape[0]
    for p in range(NJ):
        state[p, :8] = ids[p].astype(I32)
        state[p, 8:] = pids[p].astype(I32)
    at = lax.broadcasted_iota(I32, (RANK // 2, n), 0)
    row = lax.rem(lax.axis_index("x") + (at // 8) % 4, NX) * 64 + at % 8
    row = row + lax.rem(lax.axis_index("y") + at // 32, NY) * 8 + lax.axis_index("c") * 32

    def count_rows(table, owner, slot):
        looked = state[owner]
        for half in range(2):
            eight = looked[half * 8 : half * 8 + 8]
            four = jnp.where(slot == 0, eight[:4], eight[4:])
            count = jnp.where(four[0:1] == row, 1.0, 0.0)
            for k in range(1, 4):
                count = count + jnp.where(four[k : k + 1] == row, 1.0, 0.0)
            counts[table, :, half * n : (half + 1) * n] = count.astype(BF)

    slots_of(placement, used, count_rows)
    hid_s = hid[...].astype(F32).T.astype(BF)
    hgr_s = hgr[...].astype(F32).T.astype(BF)
    for pair in range(TABLES // 2):
        cols = slice(EMB + pair * 256, EMB + pair * 256 + 256)
        mixed = mm(hid_s, u[:, cols]) + bias[:, cols]
        back = mm(hgr_s, v[:, cols])
        up_float = jnp.concatenate([up[:, cols], pup[:, cols]], axis=0).astype(F32)
        pooled = (up_float * (1.0 + mixed) + back).astype(BF)
        for which in range(2):
            table = 2 * pair + which
            total = mm(counts[table], pooled[:, which * EMB : (which + 1) * EMB])
            for d in range(NY):
                outs[d][table] = total[d * 32 : (d + 1) * 32].astype(outs[d].dtype)


def total_of(refs):
    total = refs[0][...].astype(F32)
    for ref in refs[1:]:
        total = total + ref[...].astype(F32)
    return total


def table_second(*refs):
    total = total_of(refs[:NY])
    for d in range(NX):
        refs[NY + d][...] = total[:, d * 8 : (d + 1) * 8].astype(refs[NY + d].dtype)


def route_kernel(placement, *refs):
    came, outs, (held, used, at) = refs[:NX], refs[NX : NX + NY], refs[NX + NY :]
    for k in range(2 * NJ):
        at[k] = 0

    def note(table, owner, slot):
        at[2 * owner + slot] = table + 1

    slots_of(placement, used, note)
    held[0] = jnp.zeros((8, EMB), F32)
    held[1:] = total_of(came)
    for d in range(NY):
        first = lax.rem(lax.axis_index("y") + d, NY) * NZ
        for z in range(NZ):
            slots = [held[at[2 * (first + z) + s]] for s in range(2)]
            outs[d][z] = jnp.concatenate(slots, axis=0).astype(BF)


def to_z_kernel(cross, *refs):
    routed, out, sums = refs[:NY], refs[NY], refs[NY + 1]
    for k in range(cross.shape[2] // EMB):
        cols = slice(k * EMB, (k + 1) * EMB)
        total = cross[0, :, cols].astype(F32)
        for i in range(1, NX * NY):
            total = total + cross[i, :, cols].astype(F32)
        sums[:, k] = total
    for z in range(NZ):
        for d in range(NY):
            out[z, d * 16 : (d + 1) * 16] = routed[d][z]
        out[z, 64:] = sums[z].astype(BF)


def last_kernel(came, cross, table):
    scale = 1.0 / math.sqrt(EMB * 256)
    total = came[0].astype(F32)
    for z in range(1, NZ):
        total = total + came[z].astype(F32)
    for k in range(cross.shape[1] // EMB):
        cross[:, k * EMB : (k + 1) * EMB] = total[64 + k : 65 + k] * scale
    for d in range(NY):
        start = pl.multiple_of(lax.rem(lax.axis_index("y") + NY - d, NY) * 8, 8)
        for s in range(2):
            table[s, pl.ds(start, 8)] = total[d * 16 + s * 8 : d * 16 + s * 8 + 8]


def shift(chunks, axis):
    n = len(chunks)
    return [chunks[0]] + [
        lax.ppermute(chunks[d], axis, [(i, (i + d) % n) for i in range(n)]) for d in range(1, n)
    ]


def on_device(cross_input, upstream, v_weight, u_weight, bias, placement, owned_ids):
    samples, width = cross_input.shape
    blocks = 2 * width // EMB
    swap = [(0, 1), (1, 0)]
    px = lax.ppermute(cross_input, "c", swap)
    pup = lax.ppermute(upstream, "c", swap)

    (ids,) = call(ids_kernel, "ids", [((NJ, 8, EMB), I16)], owned_ids, specs=[VMEM], flops=40 << 30, size=60 << 20, vmem=4 << 20)
    ids = lax.all_to_all(ids, ("y", "z"), 0, 0, tiled=True)

    hid, hgr, cross = call(
        dense_kernel,
        "dense",
        [((RANK, 2 * samples), BF)] * 2 + [((NX * NY, NZ, 2 * width), BF)],
        cross_input,
        px,
        upstream,
        pup,
        v_weight,
        u_weight,
        specs=[VMEM] * 4 + [HBM] * 2,
        out_specs=[VMEM] * 2 + [HBM],
        scratch=[pltpu.VMEM((2 * samples, width), BF)] * 2
        + [pltpu.VMEM((RANK, width), BF)] * 2
        + [
            pltpu.VMEM((NX * NY, NZ, 2 * width), BF),
            pltpu.SemaphoreType.DMA((4,)),
            pltpu.SemaphoreType.DMA((6,)),
        ],
        vmem=50 << 20,
        flops=6 * 256 * 256 * width,
        size=6 << 20,
    )
    ids, cross = lax.optimization_barrier((ids, cross))
    cross = lax.all_to_all(cross, ("x", "y"), 0, 0, tiled=True)
    pids = lax.ppermute(ids, "c", swap)

    tables = call(
        table_kernel,
        "tables",
        [((TABLES, 32, EMB), F32)] + [((TABLES, 32, EMB), BF)] * 3,
        placement,
        hid,
        hgr,
        upstream,
        u_weight,
        v_weight,
        pup,
        bias[None],
        ids,
        pids,
        scratch=[
            pltpu.VMEM((NJ, 16, EMB), I32),
            pltpu.VMEM((TABLES, RANK // 2, 2 * samples), BF),
            pltpu.SMEM((NJ,), I32),
        ],
        vmem=40 << 20,
        flops=6 * 256 * 256 * width,
        size=9 << 20,
    )
    tables = shift(tables, "y")
    tables = call(
        table_second,
        "table_second",
        [((TABLES, 8, EMB), F32)] + [((TABLES, 8, EMB), BF)] * 3,
        *tables,
        specs=[VMEM] * 4,
        size=1 << 20,
    )
    tables = shift(tables, "x")
    routed = call(
        route_kernel,
        "route",
        [((NZ, 16, EMB), BF)] * NY,
        placement,
        *tables,
        scratch=[
            pltpu.VMEM((TABLES + 1, 8, EMB), F32),
            pltpu.SMEM((NJ,), I32),
            pltpu.SMEM((2 * NJ,), I32),
        ],
        size=1 << 20,
    )
    routed = shift(routed, "y")
    (both,) = call(
        to_z_kernel,
        "to_z",
        [((NZ, 64 + blocks, EMB), BF)],
        cross,
        *routed,
        specs=[VMEM] * (1 + NY),
        scratch=[pltpu.VMEM((NZ, blocks, EMB), F32)],
        size=3 << 20,
    )
    both = lax.all_to_all(both, "z", 0, 0, tiled=True)
    return call(
        last_kernel,
        "last",
        [((1, 2 * width), F32), ((2, NJ, EMB), F32)],
        both,
        specs=[VMEM],
        size=300000,
    )


def solution(mesh):
    fine = Mesh(mesh.devices.reshape(NX, 2, NY, NZ), ("x", "c", "y", "z"))
    grp, tbl = ("x", "c"), ("y", "z")
    in_specs = (
        P(grp + tbl, None),
        P(grp + tbl, None),
        P(),
        P(),
        P(),
        P(),
        P(tbl, None, grp),
    )
    out_specs = (P(grp + tbl, None), P(tbl, grp, None))
    return jax.shard_map(
        on_device, mesh=fine, in_specs=in_specs, out_specs=out_specs, check_vma=False
    )
```

```python
import math

import jax
import jax.numpy as jnp
from jax import lax
from jax.experimental import pallas as pl
from jax.experimental.pallas import tpu as pltpu
from jax.sharding import Mesh
from jax.sharding import PartitionSpec as P

EMB = 128
TABLES = 26
RANK = 256
NX, NY, NZ = 4, 4, 8
NJ = NY * NZ
BF = jnp.bfloat16
F32 = jnp.float32
I32 = jnp.int32
I16 = jnp.int16

VMEM = pl.BlockSpec(memory_space=pltpu.VMEM)
SMEM = pl.BlockSpec(memory_space=pltpu.SMEM)
HBM = pl.BlockSpec(memory_space=pltpu.HBM)


def nt(left, right):
    return lax.dot_general(left, right, (((1,), (1,)), ((), ())), preferred_element_type=F32)


def mm(left, right):
    return jnp.dot(left, right, preferred_element_type=F32)


def call(kernel, name, outs, *args, specs=None, out_specs=None, scratch=(), flops=0, size=0, vmem=24 << 20):
    return pl.pallas_call(
        kernel,
        out_shape=tuple(jax.ShapeDtypeStruct(shape, dtype) for shape, dtype in outs),
        in_specs=specs or [SMEM] + [VMEM] * (len(args) - 1),
        out_specs=tuple(out_specs or [VMEM] * len(outs)),
        scratch_shapes=list(scratch),
        compiler_params=pltpu.CompilerParams(vmem_limit_bytes=vmem),
        cost_estimate=pl.CostEstimate(flops=flops, bytes_accessed=size, transcendentals=0),
        name=name,
    )(*args)


def ids_kernel(ids, out):
    for j in range(NJ):
        parts = [ids[s, :, j * EMB : (j + 1) * EMB] for s in range(2)]
        out[j] = jnp.concatenate(parts, axis=0).astype(I16)


def dense_kernel(x, px, up, pup, v_in, u_in, hid, hgr, by_x, *refs):
    by_y, (both, prod, v, u, held, held_y, in_sems, sems) = refs[:4], refs[4:]
    n, width = x.shape
    loads = []
    for source, target in ((v_in, v), (u_in, u)):
        for k in range(2):
            rows = slice(k * 128, (k + 1) * 128)
            loads.append(
                pltpu.make_async_copy(source.at[rows], target.at[rows], in_sems.at[len(loads)])
            )
            loads[-1].start()
    both[:n] = x[...]
    both[n:] = px[...]
    prod[:n] = (x[...].astype(F32) * up[...].astype(F32)).astype(BF)
    prod[n:] = (px[...].astype(F32) * pup[...].astype(F32)).astype(BF)
    loads[0].wait()
    loads[1].wait()
    hid[...] = nt(v[...], both[...]).astype(BF)
    loads[2].wait()
    loads[3].wait()
    hgr[...] = nt(u[...], prod[...]).astype(BF)
    at = lax.broadcasted_iota(I32, (RANK // 2, RANK), 0)
    row = lax.broadcasted_iota(I32, (RANK // 2, RANK), 1)
    base = lax.axis_index("c") * 32 + at % 8
    to_x, to_y = lax.axis_index("x"), lax.axis_index("y")
    row_x = base + (at // 32) * 64 + lax.rem(to_y + (at // 8) % 4, NY) * 8
    row_y = base + lax.rem(to_x + (at // 8) % 4, NX) * 64 + lax.rem(to_y + at // 32, NY) * 8
    hid_own = mm((row == row_x).astype(F32).astype(BF), hid[...]).astype(BF)
    hgr_own = mm((row == row_y).astype(F32).astype(BF), hgr[...]).astype(BF)
    step = 1152
    copies = []
    for k in range(width // step):
        cols = slice(k * step, (k + 1) * step)
        total = mm(hgr_own, both[:, cols])
        for d in range(4):
            held_y[d, :, cols] = total[d * 32 : (d + 1) * 32].astype(BF)
    for d in range(4):
        copies.append(pltpu.make_async_copy(held_y.at[d], by_y[d], sems.at[d]))
        copies[-1].start()
    for k in range(width // step):
        cols = slice(k * step, (k + 1) * step)
        total = mm(hid_own, prod[:, cols])
        for i in range(NX):
            held[i, :, cols] = total[i * 32 : (i + 1) * 32].astype(BF)
        copies.append(
            pltpu.make_async_copy(held.at[:, :, cols], by_x.at[:, :, cols], sems.at[4 + k])
        )
        copies[-1].start()
    for copy in copies:
        copy.wait()


def slots_of(placement, used, visit):
    for j in range(NJ):
        used[j] = 0
    for table in range(TABLES):
        owner = placement[table]
        slot = used[owner]
        used[owner] = slot + 1
        visit(table, owner, slot)


def table_kernel(placement, hid, hgr, up, u, v, pup, bias, ids, pids, *refs):
    out, state, counts, used = refs
    n = up.shape[0]
    for p in range(NJ):
        state[p, :8] = ids[p].astype(I32)
        state[p, 8:] = pids[p].astype(I32)
    at = lax.broadcasted_iota(I32, (RANK // 2, n), 0)
    row = (at // 32) * 64 + lax.axis_index("c") * 32 + at % 32

    def count_rows(table, owner, slot):
        looked = state[owner]
        for half in range(2):
            eight = looked[half * 8 : half * 8 + 8]
            four = jnp.where(slot == 0, eight[:4], eight[4:])
            count = jnp.where(four[0:1] == row, 1.0, 0.0)
            for k in range(1, 4):
                count = count + jnp.where(four[k : k + 1] == row, 1.0, 0.0)
            counts[table, :, half * n : (half + 1) * n] = count.astype(BF)

    slots_of(placement, used, count_rows)
    hid_s = hid[...].astype(F32).T.astype(BF)
    hgr_s = hgr[...].astype(F32).T.astype(BF)
    for pair in range(TABLES // 2):
        cols = slice(EMB + pair * 256, EMB + pair * 256 + 256)
        mixed = mm(hid_s, u[:, cols]) + bias[:, cols]
        back = mm(hgr_s, v[:, cols])
        up_float = jnp.concatenate([up[:, cols], pup[:, cols]], axis=0).astype(F32)
        pooled = (up_float * (1.0 + mixed) + back).astype(BF)
        for which in range(2):
            table = 2 * pair + which
            total = mm(counts[table], pooled[:, which * EMB : (which + 1) * EMB])
            for k in range(NX * NY):
                out[k, table] = total[k * 8 : (k + 1) * 8].astype(BF)


def total_of(refs):
    total = refs[0][...].astype(F32)
    for ref in refs[1:]:
        total = total + ref[...].astype(F32)
    return total


def cross_second(*refs):
    came_x, came_y, outs = refs[0], refs[1:5], refs[5:]
    total = came_x[0].astype(F32)
    for i in range(1, NX):
        total = total + came_x[i].astype(F32)
    for d in range(4):
        outs[d][...] = total[d * 8 : (d + 1) * 8].astype(outs[d].dtype)
    total = total_of(came_y)
    for d in range(4):
        outs[4 + d][...] = total[d * 8 : (d + 1) * 8].astype(outs[4 + d].dtype)


def route_kernel(placement, *refs):
    came, outs, (held, used, at) = refs[0], refs[1 : 1 + NY], refs[1 + NY :]
    for k in range(2 * NJ):
        at[k] = 0

    def note(table, owner, slot):
        at[2 * owner + slot] = table + 1

    slots_of(placement, used, note)
    held[0] = jnp.zeros((8, EMB), F32)
    total = came[0].astype(F32)
    for k in range(1, NX * NY):
        total = total + came[k].astype(F32)
    held[1:] = total
    for d in range(NY):
        first = lax.rem(lax.axis_index("y") + d, NY) * NZ
        for z in range(NZ):
            slots = [held[at[2 * (first + z) + s]] for s in range(2)]
            outs[d][z] = jnp.concatenate(slots, axis=0).astype(BF)


def to_z_kernel(*refs):
    cross, routed, out, sums = refs[:8], refs[8 : 8 + NY], refs[8 + NY], refs[9 + NY]
    blocks = cross[0].shape[1] // EMB
    for side in range(2):
        total = total_of(cross[4 * side : 4 * side + 4])
        for k in range(blocks):
            sums[:, side * blocks + k] = total[:, k * EMB : (k + 1) * EMB]
    for z in range(NZ):
        for d in range(NY):
            out[z, d * 16 : (d + 1) * 16] = routed[d][z]
        out[z, 64:] = sums[z].astype(BF)


def last_kernel(came, cross, table):
    scale = 1.0 / math.sqrt(EMB * 256)
    total = came[0].astype(F32)
    for z in range(1, NZ):
        total = total + came[z].astype(F32)
    for k in range(cross.shape[1] // EMB):
        cross[:, k * EMB : (k + 1) * EMB] = total[64 + k : 65 + k] * scale
    for d in range(NY):
        start = pl.multiple_of(lax.rem(lax.axis_index("y") + NY - d, NY) * 8, 8)
        for s in range(2):
            table[s, pl.ds(start, 8)] = total[d * 16 + s * 8 : d * 16 + s * 8 + 8]


def shift(chunks, axis):
    n = len(chunks)
    return [chunks[0]] + [
        lax.ppermute(chunks[d], axis, [(i, (i + d) % n) for i in range(n)]) for d in range(1, n)
    ]


def on_device(cross_input, upstream, v_weight, u_weight, bias, placement, owned_ids):
    samples, width = cross_input.shape
    blocks = 2 * width // EMB
    swap = [(0, 1), (1, 0)]
    px = lax.ppermute(cross_input, "c", swap)
    pup = lax.ppermute(upstream, "c", swap)

    (ids,) = call(ids_kernel, "ids", [((NJ, 8, EMB), I16)], owned_ids, specs=[VMEM], flops=40 << 30, size=60 << 20, vmem=4 << 20)
    ids = lax.all_to_all(ids, ("y", "z"), 0, 0, tiled=True)

    sent = [((NJ, width), BF)] * 4
    hid, hgr, by_x, *by_y = call(
        dense_kernel,
        "dense",
        [((RANK, 2 * samples), BF)] * 2 + [((NX, NJ, width), BF)] + sent,
        cross_input,
        px,
        upstream,
        pup,
        v_weight,
        u_weight,
        specs=[VMEM] * 4 + [HBM] * 2,
        out_specs=[VMEM] * 2 + [HBM] * 5,
        scratch=[pltpu.VMEM((2 * samples, width), BF)] * 2
        + [pltpu.VMEM((RANK, width), BF)] * 2
        + [
            pltpu.VMEM((NX, NJ, width), BF),
            pltpu.VMEM((NY, NJ, width), BF),
            pltpu.SemaphoreType.DMA((4,)),
            pltpu.SemaphoreType.DMA((7,)),
        ],
        vmem=57 << 20,
        flops=6 * 256 * 256 * width,
        size=6 << 20,
    )
    by_y = shift(by_y, "y")
    ids, by_x = lax.optimization_barrier((ids, by_x))
    by_x = lax.all_to_all(by_x, "x", 0, 0, tiled=True)
    hid, *by_y = lax.optimization_barrier((hid, *by_y))
    pids = lax.ppermute(ids, "c", swap)

    (tables,) = call(
        table_kernel,
        "tables",
        [((NX * NY, TABLES, 8, EMB), BF)],
        placement,
        hid,
        hgr,
        upstream,
        u_weight,
        v_weight,
        pup,
        bias[None],
        ids,
        pids,
        scratch=[
            pltpu.VMEM((NJ, 16, EMB), I32),
            pltpu.VMEM((TABLES, RANK // 2, 2 * samples), BF),
            pltpu.SMEM((NJ,), I32),
        ],
        vmem=40 << 20,
        flops=6 * 256 * 256 * width,
        size=9 << 20,
    )
    by_x, tables = lax.optimization_barrier((by_x, tables))
    tables = lax.all_to_all(tables, ("x", "y"), 0, 0, tiled=True)
    sent = [((NZ, width), F32)] + [((NZ, width), BF)] * 3
    cross = call(
        cross_second,
        "cross_second",
        sent * 2,
        by_x,
        *by_y,
        specs=[VMEM] * 5,
        size=3 << 20,
    )
    cross = shift(cross[:4], "y") + shift(cross[4:], "x")
    routed = call(
        route_kernel,
        "route",
        [((NZ, 16, EMB), BF)] * NY,
        placement,
        tables,
        scratch=[
            pltpu.VMEM((TABLES + 1, 8, EMB), F32),
            pltpu.SMEM((NJ,), I32),
            pltpu.SMEM((2 * NJ,), I32),
        ],
        size=1 << 20,
    )
    routed = shift(routed, "y")
    (both,) = call(
        to_z_kernel,
        "to_z",
        [((NZ, 64 + blocks, EMB), BF)],
        *cross,
        *routed,
        specs=[VMEM] * (8 + NY),
        scratch=[pltpu.VMEM((NZ, blocks, EMB), F32)],
        size=3 << 20,
    )
    both = lax.all_to_all(both, "z", 0, 0, tiled=True)
    return call(
        last_kernel,
        "last",
        [((1, 2 * width), F32), ((2, NJ, EMB), F32)],
        both,
        specs=[VMEM],
        size=300000,
    )


def solution(mesh):
    fine = Mesh(mesh.devices.reshape(NX, 2, NY, NZ), ("x", "c", "y", "z"))
    grp, tbl = ("x", "c"), ("y", "z")
    in_specs = (
        P(grp + tbl, None),
        P(grp + tbl, None),
        P(),
        P(),
        P(),
        P(),
        P(tbl, None, grp),
    )
    out_specs = (P(grp + tbl, None), P(tbl, grp, None))
    return jax.shard_map(
        on_device, mesh=fine, in_specs=in_specs, out_specs=out_specs, check_vma=False
    )
```

```python
import math

import jax
import jax.numpy as jnp
from jax import lax
from jax.experimental import pallas as pl
from jax.experimental.pallas import tpu as pltpu
from jax.sharding import Mesh
from jax.sharding import PartitionSpec as P

EMB = 128
TABLES = 26
RANK = 256
NX, NY, NZ = 4, 4, 8
NJ = NY * NZ
BF = jnp.bfloat16
F32 = jnp.float32
I32 = jnp.int32
I16 = jnp.int16

VMEM = pl.BlockSpec(memory_space=pltpu.VMEM)
SMEM = pl.BlockSpec(memory_space=pltpu.SMEM)
HBM = pl.BlockSpec(memory_space=pltpu.HBM)


def nt(left, right):
    return lax.dot_general(left, right, (((1,), (1,)), ((), ())), preferred_element_type=F32)


def mm(left, right):
    return jnp.dot(left, right, preferred_element_type=F32)


def call(kernel, name, outs, *args, specs=None, out_specs=None, scratch=(), flops=0, size=0, vmem=24 << 20):
    return pl.pallas_call(
        kernel,
        out_shape=tuple(jax.ShapeDtypeStruct(shape, dtype) for shape, dtype in outs),
        in_specs=specs or [SMEM] + [VMEM] * (len(args) - 1),
        out_specs=tuple(out_specs or [VMEM] * len(outs)),
        scratch_shapes=list(scratch),
        compiler_params=pltpu.CompilerParams(vmem_limit_bytes=vmem),
        cost_estimate=pl.CostEstimate(flops=flops, bytes_accessed=size, transcendentals=0),
        name=name,
    )(*args)


def ids_kernel(ids, out):
    for j in range(NJ):
        parts = [ids[s, :, j * EMB : (j + 1) * EMB] for s in range(2)]
        out[j] = jnp.concatenate(parts, axis=0).astype(I16)


def own_rows(full, core):
    picks = [
        jnp.where(core == 0, full[i * 64 : i * 64 + 32], full[i * 64 + 32 : i * 64 + 64])
        for i in range(NX)
    ]
    return jnp.concatenate(picks, axis=0)


def dense_kernel(x, px, up, pup, v_in, u_in, hid, hgr, out, both, prod, v, u, held, in_sems, sems):
    n, width = x.shape
    core = lax.axis_index("c")
    loads = []
    for source, target in ((v_in, v), (u_in, u)):
        for k in range(2):
            rows = slice(k * 128, (k + 1) * 128)
            loads.append(
                pltpu.make_async_copy(source.at[rows], target.at[rows], in_sems.at[len(loads)])
            )
            loads[-1].start()
    both[:n] = x[...]
    both[n:] = px[...]
    prod[:n] = (x[...].astype(F32) * up[...].astype(F32)).astype(BF)
    prod[n:] = (px[...].astype(F32) * pup[...].astype(F32)).astype(BF)
    loads[0].wait()
    loads[1].wait()
    hid[...] = nt(v[...], both[...]).astype(BF)
    loads[2].wait()
    loads[3].wait()
    hgr[...] = nt(u[...], prod[...]).astype(BF)
    hid_own = own_rows(hid[...].astype(F32), core).astype(BF)
    hgr_own = own_rows(hgr[...].astype(F32), core).astype(BF)
    step = 1152
    copies = []
    for side, (left, right) in enumerate(((hid_own, prod), (hgr_own, both))):
        for k in range(width // step):
            total = mm(left, right[:, k * step : (k + 1) * step])
            cols = slice(side * width + k * step, side * width + (k + 1) * step)
            for i in range(NX):
                held[i, :, cols] = total[i * NJ : (i + 1) * NJ].astype(BF)
            copies.append(
                pltpu.make_async_copy(
                    held.at[:, :, cols], out.at[:, :, cols], sems.at[len(copies)]
                )
            )
            copies[-1].start()
    for copy in copies:
        copy.wait()


def slots_of(placement, used, visit):
    for j in range(NJ):
        used[j] = 0
    for table in range(TABLES):
        owner = placement[table]
        slot = used[owner]
        used[owner] = slot + 1
        visit(table, owner, slot)


def table_kernel(placement, hid, hgr, up, u, v, pup, bias, ids, pids, *refs):
    outs, (state, counts, used) = refs[:4], refs[4:]
    n = up.shape[0]
    for p in range(NJ):
        state[p, :8] = ids[p].astype(I32)
        state[p, 8:] = pids[p].astype(I32)
    at = lax.broadcasted_iota(I32, (RANK // 2, n), 0)
    row = lax.rem(lax.axis_index("x") + (at // 8) % 4, NX) * 64 + at % 8
    row = row + lax.rem(lax.axis_index("y") + at // 32, NY) * 8 + lax.axis_index("c") * 32

    def count_rows(table, owner, slot):
        looked = state[owner]
        for half in range(2):
            eight = looked[half * 8 : half * 8 + 8]
            four = jnp.where(slot == 0, eight[:4], eight[4:])
            count = jnp.where(four[0:1] == row, 1.0, 0.0)
            for k in range(1, 4):
                count = count + jnp.where(four[k : k + 1] == row, 1.0, 0.0)
            counts[table, :, half * n : (half + 1) * n] = count.astype(BF)

    slots_of(placement, used, count_rows)
    hid_s = hid[...].astype(F32).T.astype(BF)
    hgr_s = hgr[...].astype(F32).T.astype(BF)
    for pair in range(TABLES // 2):
        cols = slice(EMB + pair * 256, EMB + pair * 256 + 256)
        mixed = mm(hid_s, u[:, cols]) + bias[:, cols]
        back = mm(hgr_s, v[:, cols])
        up_float = jnp.concatenate([up[:, cols], pup[:, cols]], axis=0).astype(F32)
        pooled = (up_float * (1.0 + mixed) + back).astype(BF)
        for which in range(2):
            table = 2 * pair + which
            total = mm(counts[table], pooled[:, which * EMB : (which + 1) * EMB])
            for d in range(NY):
                outs[d][table] = total[d * 32 : (d + 1) * 32].astype(outs[d].dtype)


def total_of(refs):
    total = refs[0][...].astype(F32)
    for ref in refs[1:]:
        total = total + ref[...].astype(F32)
    return total


def table_second(*refs):
    total = total_of(refs[:NY])
    for d in range(NX):
        refs[NY + d][...] = total[:, d * 8 : (d + 1) * 8].astype(refs[NY + d].dtype)


def cross_kernel(came, out, sums):
    for k in range(came.shape[2] // EMB):
        cols = slice(k * EMB, (k + 1) * EMB)
        total = came[0, :, cols].astype(F32)
        for i in range(1, NX):
            total = total + came[i, :, cols].astype(F32)
        sums[:, k] = total
    for j in range(NJ):
        out[j] = sums[j].astype(BF)


def route_kernel(placement, cross, *refs):
    came, out, (held, used, at) = refs[:NX], refs[NX], refs[NX + 1 :]
    for k in range(2 * NJ):
        at[k] = 0

    def note(table, owner, slot):
        at[2 * owner + slot] = table + 1

    slots_of(placement, used, note)
    held[0] = jnp.zeros((8, EMB), F32)
    held[1:] = total_of(came)
    for j in range(NJ):
        slots = [held[at[2 * j + s]] for s in range(2)]
        out[j, :16] = jnp.concatenate(slots, axis=0).astype(BF)
        out[j, 16:] = cross[j]


def last_kernel(came, cross, table):
    scale = 1.0 / math.sqrt(EMB * 256)
    total = came[0, 16:].astype(F32)
    for j in range(1, NJ):
        total = total + came[j, 16:].astype(F32)
    for k in range(cross.shape[1] // EMB):
        cross[:, k * EMB : (k + 1) * EMB] = total[k : k + 1] * scale
    for y in range(NY):
        rows = came[y * NZ, :16].astype(F32)
        for z in range(1, NZ):
            rows = rows + came[y * NZ + z, :16].astype(F32)
        for s in range(2):
            table[s, y * 8 : (y + 1) * 8] = rows[s * 8 : (s + 1) * 8]


def shift(chunks, axis):
    n = len(chunks)
    return [chunks[0]] + [
        lax.ppermute(chunks[d], axis, [(i, (i + d) % n) for i in range(n)]) for d in range(1, n)
    ]


def on_device(cross_input, upstream, v_weight, u_weight, bias, placement, owned_ids):
    samples, width = cross_input.shape
    blocks = 2 * width // EMB
    swap = [(0, 1), (1, 0)]
    px = lax.ppermute(cross_input, "c", swap)
    pup = lax.ppermute(upstream, "c", swap)

    (ids,) = call(ids_kernel, "ids", [((NJ, 8, EMB), I16)], owned_ids, specs=[VMEM], flops=40 << 30, size=60 << 20, vmem=4 << 20)
    ids = lax.all_to_all(ids, ("y", "z"), 0, 0, tiled=True)

    hid, hgr, cross = call(
        dense_kernel,
        "dense",
        [((RANK, 2 * samples), BF)] * 2 + [((NX, NJ, 2 * width), BF)],
        cross_input,
        px,
        upstream,
        pup,
        v_weight,
        u_weight,
        specs=[VMEM] * 4 + [HBM] * 2,
        out_specs=[VMEM] * 2 + [HBM],
        scratch=[pltpu.VMEM((2 * samples, width), BF)] * 2
        + [pltpu.VMEM((RANK, width), BF)] * 2
        + [
            pltpu.VMEM((NX, NJ, 2 * width), BF),
            pltpu.SemaphoreType.DMA((4,)),
            pltpu.SemaphoreType.DMA((6,)),
        ],
        vmem=50 << 20,
        flops=6 * 256 * 256 * width,
        size=6 << 20,
    )
    ids, cross = lax.optimization_barrier((ids, cross))
    cross = lax.all_to_all(cross, "x", 0, 0, tiled=True)
    pids = lax.ppermute(ids, "c", swap)

    tables = call(
        table_kernel,
        "tables",
        [((TABLES, 32, EMB), F32)] + [((TABLES, 32, EMB), BF)] * 3,
        placement,
        hid,
        hgr,
        upstream,
        u_weight,
        v_weight,
        pup,
        bias[None],
        ids,
        pids,
        scratch=[
            pltpu.VMEM((NJ, 16, EMB), I32),
            pltpu.VMEM((TABLES, RANK // 2, 2 * samples), BF),
            pltpu.SMEM((NJ,), I32),
        ],
        vmem=40 << 20,
        flops=6 * 256 * 256 * width,
        size=9 << 20,
    )
    tables = shift(tables, "y")
    tables = call(
        table_second,
        "table_second",
        [((TABLES, 8, EMB), F32)] + [((TABLES, 8, EMB), BF)] * 3,
        *tables,
        specs=[VMEM] * 4,
        size=1 << 20,
    )
    tables = shift(tables, "x")
    (cross,) = call(
        cross_kernel,
        "cross_sum",
        [((NJ, blocks, EMB), BF)],
        cross,
        specs=[VMEM],
        scratch=[pltpu.VMEM((NJ, blocks, EMB), F32)],
        size=3 << 20,
    )
    (routed,) = call(
        route_kernel,
        "route",
        [((NJ, 16 + blocks, EMB), BF)],
        placement,
        cross,
        *tables,
        scratch=[
            pltpu.VMEM((TABLES + 1, 8, EMB), F32),
            pltpu.SMEM((NJ,), I32),
            pltpu.SMEM((2 * NJ,), I32),
        ],
        size=2 << 20,
    )
    routed = lax.all_to_all(routed, ("y", "z"), 0, 0, tiled=True)
    return call(
        last_kernel,
        "last",
        [((1, 2 * width), F32), ((2, NJ, EMB), F32)],
        routed,
        specs=[VMEM],
        size=1 << 20,
    )


def solution(mesh):
    fine = Mesh(mesh.devices.reshape(NX, 2, NY, NZ), ("x", "c", "y", "z"))
    grp, tbl = ("x", "c"), ("y", "z")
    in_specs = (
        P(grp + tbl, None),
        P(grp + tbl, None),
        P(),
        P(),
        P(),
        P(),
        P(tbl, None, grp),
    )
    out_specs = (P(grp + tbl, None), P(tbl, grp, None))
    return jax.shard_map(
        on_device, mesh=fine, in_specs=in_specs, out_specs=out_specs, check_vma=False
    )
```

```python
import math

import jax
import jax.numpy as jnp
from jax import lax
from jax.experimental import pallas as pl
from jax.experimental.pallas import tpu as pltpu
from jax.sharding import Mesh
from jax.sharding import PartitionSpec as P

EMB = 128
TABLES = 26
RANK = 256
NX, NY, NZ = 4, 4, 8
NJ = NY * NZ
BF = jnp.bfloat16
F32 = jnp.float32
I32 = jnp.int32
I16 = jnp.int16

VMEM = pl.BlockSpec(memory_space=pltpu.VMEM)
SMEM = pl.BlockSpec(memory_space=pltpu.SMEM)
HBM = pl.BlockSpec(memory_space=pltpu.HBM)


def nt(left, right):
    return lax.dot_general(left, right, (((1,), (1,)), ((), ())), preferred_element_type=F32)


def mm(left, right):
    return jnp.dot(left, right, preferred_element_type=F32)


def call(kernel, name, outs, *args, specs=None, out_specs=None, scratch=(), flops=0, size=0, vmem=24 << 20):
    return pl.pallas_call(
        kernel,
        out_shape=tuple(jax.ShapeDtypeStruct(shape, dtype) for shape, dtype in outs),
        in_specs=specs or [SMEM] + [VMEM] * (len(args) - 1),
        out_specs=tuple(out_specs or [VMEM] * len(outs)),
        scratch_shapes=list(scratch),
        compiler_params=pltpu.CompilerParams(vmem_limit_bytes=vmem),
        cost_estimate=pl.CostEstimate(flops=flops, bytes_accessed=size, transcendentals=0),
        name=name,
    )(*args)


def ids_kernel(ids, out):
    for j in range(NJ):
        parts = [ids[s, :, j * EMB : (j + 1) * EMB] for s in range(2)]
        out[j] = jnp.concatenate(parts, axis=0).astype(I16)


def own_rows(full, core):
    picks = [
        jnp.where(core == 0, full[i * 64 : i * 64 + 32], full[i * 64 + 32 : i * 64 + 64])
        for i in range(NX)
    ]
    return jnp.concatenate(picks, axis=0)


def dense_kernel(x, px, up, pup, v_in, u_in, bias, out, pooled, both, prod, v, u, held, held_p, in_sems, sems):
    n, width = x.shape
    core = lax.axis_index("c")
    loads = []
    for source, target in ((v_in, v), (u_in, u)):
        for k in range(2):
            rows = slice(k * 128, (k + 1) * 128)
            loads.append(
                pltpu.make_async_copy(source.at[rows], target.at[rows], in_sems.at[len(loads)])
            )
            loads[-1].start()
    both[:n] = x[...]
    both[n:] = px[...]
    prod[:n] = (x[...].astype(F32) * up[...].astype(F32)).astype(BF)
    prod[n:] = (px[...].astype(F32) * pup[...].astype(F32)).astype(BF)
    loads[0].wait()
    loads[1].wait()
    hid = nt(v[...], both[...]).astype(BF)
    loads[2].wait()
    loads[3].wait()
    hgr = nt(u[...], prod[...]).astype(BF)
    hid_own = own_rows(hid.astype(F32), core).astype(BF)
    hgr_own = own_rows(hgr.astype(F32), core).astype(BF)
    step = 1152
    copies = []
    for side, (left, right) in enumerate(((hid_own, prod), (hgr_own, both))):
        for k in range(width // step):
            total = mm(left, right[:, k * step : (k + 1) * step])
            cols = slice(side * width + k * step, side * width + (k + 1) * step)
            for i in range(NX):
                held[i, :, cols] = total[i * NJ : (i + 1) * NJ].astype(BF)
            copies.append(
                pltpu.make_async_copy(
                    held.at[:, :, cols], out.at[:, :, cols], sems.at[len(copies)]
                )
            )
            copies[-1].start()
    hid_s = hid.astype(F32).T.astype(BF)
    hgr_s = hgr.astype(F32).T.astype(BF)
    for pair in range(TABLES // 2):
        cols = slice(EMB + pair * 256, EMB + pair * 256 + 256)
        mixed = mm(hid_s, u[:, cols]) + bias[cols].reshape(1, 256)
        back = mm(hgr_s, v[:, cols])
        up_float = jnp.concatenate([up[:, cols], pup[:, cols]], axis=0).astype(F32)
        held_p[:, pair * 256 : pair * 256 + 256] = (up_float * (1.0 + mixed) + back).astype(BF)
    copies.append(pltpu.make_async_copy(held_p, pooled, sems.at[len(copies)]))
    copies[-1].start()
    for copy in copies:
        copy.wait()


def slots_of(placement, used, visit):
    for j in range(NJ):
        used[j] = 0
    for table in range(TABLES):
        owner = placement[table]
        slot = used[owner]
        used[owner] = slot + 1
        visit(table, owner, slot)


def table_kernel(placement, pooled, ids, pids, *refs):
    outs, (state, counts, used) = refs[:4], refs[4:]
    n = ids.shape[2]
    for p in range(NJ):
        state[p, :8] = ids[p].astype(I32)
        state[p, 8:] = pids[p].astype(I32)
    at = lax.broadcasted_iota(I32, (RANK // 2, n), 0)
    row = lax.rem(lax.axis_index("x") + (at // 8) % 4, NX) * 64 + at % 8
    row = row + lax.rem(lax.axis_index("y") + at // 32, NY) * 8 + lax.axis_index("c") * 32

    def count_rows(table, owner, slot):
        looked = state[owner]
        for half in range(2):
            eight = looked[half * 8 : half * 8 + 8]
            four = jnp.where(slot == 0, eight[:4], eight[4:])
            count = jnp.where(four[0:1] == row, 1.0, 0.0)
            for k in range(1, 4):
                count = count + jnp.where(four[k : k + 1] == row, 1.0, 0.0)
            counts[table, :, half * n : (half + 1) * n] = count.astype(BF)

    slots_of(placement, used, count_rows)
    for table in range(TABLES):
        total = mm(counts[table], pooled[:, table * EMB : (table + 1) * EMB])
        for d in range(NY):
            outs[d][table] = total[d * 32 : (d + 1) * 32].astype(outs[d].dtype)


def total_of(refs):
    total = refs[0][...].astype(F32)
    for ref in refs[1:]:
        total = total + ref[...].astype(F32)
    return total


def table_second(*refs):
    total = total_of(refs[:NY])
    for d in range(NX):
        refs[NY + d][...] = total[:, d * 8 : (d + 1) * 8].astype(refs[NY + d].dtype)


def cross_kernel(came, out, sums):
    for k in range(came.shape[2] // EMB):
        cols = slice(k * EMB, (k + 1) * EMB)
        total = came[0, :, cols].astype(F32)
        for i in range(1, NX):
            total = total + came[i, :, cols].astype(F32)
        sums[:, k] = total
    for j in range(NJ):
        out[j] = sums[j].astype(BF)


def route_kernel(placement, cross, *refs):
    came, out, (held, used, at) = refs[:NX], refs[NX], refs[NX + 1 :]
    for k in range(2 * NJ):
        at[k] = 0

    def note(table, owner, slot):
        at[2 * owner + slot] = table + 1

    slots_of(placement, used, note)
    held[0] = jnp.zeros((8, EMB), F32)
    held[1:] = total_of(came)
    for j in range(NJ):
        slots = [held[at[2 * j + s]] for s in range(2)]
        out[j, :16] = jnp.concatenate(slots, axis=0).astype(BF)
        out[j, 16:] = cross[j]


def last_kernel(came, cross, table):
    scale = 1.0 / math.sqrt(EMB * 256)
    total = came[0, 16:].astype(F32)
    for j in range(1, NJ):
        total = total + came[j, 16:].astype(F32)
    for k in range(cross.shape[1] // EMB):
        cross[:, k * EMB : (k + 1) * EMB] = total[k : k + 1] * scale
    for y in range(NY):
        rows = came[y * NZ, :16].astype(F32)
        for z in range(1, NZ):
            rows = rows + came[y * NZ + z, :16].astype(F32)
        for s in range(2):
            table[s, y * 8 : (y + 1) * 8] = rows[s * 8 : (s + 1) * 8]


def shift(chunks, axis):
    n = len(chunks)
    return [chunks[0]] + [
        lax.ppermute(chunks[d], axis, [(i, (i + d) % n) for i in range(n)]) for d in range(1, n)
    ]


def on_device(cross_input, upstream, v_weight, u_weight, bias, placement, owned_ids):
    samples, width = cross_input.shape
    blocks = 2 * width // EMB
    swap = [(0, 1), (1, 0)]
    px = lax.ppermute(cross_input, "c", swap)
    pup = lax.ppermute(upstream, "c", swap)

    (ids,) = call(ids_kernel, "ids", [((NJ, 8, EMB), I16)], owned_ids, specs=[VMEM], flops=40 << 30, size=60 << 20, vmem=4 << 20)
    ids = lax.all_to_all(ids, ("y", "z"), 0, 0, tiled=True)

    cross, pooled = call(
        dense_kernel,
        "dense",
        [((NX, NJ, 2 * width), BF), ((2 * samples, TABLES * EMB), BF)],
        cross_input,
        px,
        upstream,
        pup,
        v_weight,
        u_weight,
        bias,
        specs=[VMEM] * 4 + [HBM] * 2 + [VMEM],
        out_specs=[HBM] * 2,
        scratch=[pltpu.VMEM((2 * samples, width), BF)] * 2
        + [pltpu.VMEM((RANK, width), BF)] * 2
        + [
            pltpu.VMEM((NX, NJ, 2 * width), BF),
            pltpu.VMEM((2 * samples, TABLES * EMB), BF),
            pltpu.SemaphoreType.DMA((4,)),
            pltpu.SemaphoreType.DMA((7,)),
        ],
        vmem=50 << 20,
        flops=6 * 256 * 256 * width,
        size=6 << 20,
    )
    ids, cross = lax.optimization_barrier((ids, cross))
    cross = lax.all_to_all(cross, "x", 0, 0, tiled=True)
    pids = lax.ppermute(ids, "c", swap)

    tables = call(
        table_kernel,
        "tables",
        [((TABLES, 32, EMB), F32)] + [((TABLES, 32, EMB), BF)] * 3,
        placement,
        pooled,
        ids,
        pids,
        scratch=[
            pltpu.VMEM((NJ, 16, EMB), I32),
            pltpu.VMEM((TABLES, RANK // 2, 2 * samples), BF),
            pltpu.SMEM((NJ,), I32),
        ],
        vmem=40 << 20,
        flops=6 * 256 * 256 * width,
        size=9 << 20,
    )
    tables = shift(tables, "y")
    tables = call(
        table_second,
        "table_second",
        [((TABLES, 8, EMB), F32)] + [((TABLES, 8, EMB), BF)] * 3,
        *tables,
        specs=[VMEM] * 4,
        size=1 << 20,
    )
    tables = shift(tables, "x")
    (cross,) = call(
        cross_kernel,
        "cross_sum",
        [((NJ, blocks, EMB), BF)],
        cross,
        specs=[VMEM],
        scratch=[pltpu.VMEM((NJ, blocks, EMB), F32)],
        size=3 << 20,
    )
    (routed,) = call(
        route_kernel,
        "route",
        [((NJ, 16 + blocks, EMB), BF)],
        placement,
        cross,
        *tables,
        scratch=[
            pltpu.VMEM((TABLES + 1, 8, EMB), F32),
            pltpu.SMEM((NJ,), I32),
            pltpu.SMEM((2 * NJ,), I32),
        ],
        size=2 << 20,
    )
    routed = lax.all_to_all(routed, ("y", "z"), 0, 0, tiled=True)
    return call(
        last_kernel,
        "last",
        [((1, 2 * width), F32), ((2, NJ, EMB), F32)],
        routed,
        specs=[VMEM],
        size=1 << 20,
    )


def solution(mesh):
    fine = Mesh(mesh.devices.reshape(NX, 2, NY, NZ), ("x", "c", "y", "z"))
    grp, tbl = ("x", "c"), ("y", "z")
    in_specs = (
        P(grp + tbl, None),
        P(grp + tbl, None),
        P(),
        P(),
        P(),
        P(),
        P(tbl, None, grp),
    )
    out_specs = (P(grp + tbl, None), P(tbl, grp, None))
    return jax.shard_map(
        on_device, mesh=fine, in_specs=in_specs, out_specs=out_specs, check_vma=False
    )
```

```python
import math

import jax
import jax.numpy as jnp
from jax import lax
from jax.experimental import pallas as pl
from jax.experimental.pallas import tpu as pltpu
from jax.sharding import Mesh
from jax.sharding import PartitionSpec as P

EMB = 128
TABLES = 26
RANK = 256
NX, NY, NZ = 4, 4, 8
NJ = NY * NZ
BF = jnp.bfloat16
F32 = jnp.float32
I32 = jnp.int32
I16 = jnp.int16

VMEM = pl.BlockSpec(memory_space=pltpu.VMEM)
SMEM = pl.BlockSpec(memory_space=pltpu.SMEM)
HBM = pl.BlockSpec(memory_space=pltpu.HBM)


def nt(left, right):
    return lax.dot_general(left, right, (((1,), (1,)), ((), ())), preferred_element_type=F32)


def mm(left, right):
    return jnp.dot(left, right, preferred_element_type=F32)


def call(kernel, name, outs, *args, specs=None, out_specs=None, scratch=(), flops=0, size=0, vmem=24 << 20):
    return pl.pallas_call(
        kernel,
        out_shape=tuple(jax.ShapeDtypeStruct(shape, dtype) for shape, dtype in outs),
        in_specs=specs or [SMEM] + [VMEM] * (len(args) - 1),
        out_specs=tuple(out_specs or [VMEM] * len(outs)),
        scratch_shapes=list(scratch),
        compiler_params=pltpu.CompilerParams(vmem_limit_bytes=vmem),
        cost_estimate=pl.CostEstimate(flops=flops, bytes_accessed=size, transcendentals=0),
        name=name,
    )(*args)


def ids_kernel(ids, out):
    for j in range(NJ):
        parts = [ids[s, :, j * EMB : (j + 1) * EMB] for s in range(2)]
        out[j] = jnp.concatenate(parts, axis=0).astype(I16)


def own_rows(full, core):
    picks = [
        jnp.where(core == 0, full[i * 64 : i * 64 + 32], full[i * 64 + 32 : i * 64 + 64])
        for i in range(NX)
    ]
    return jnp.concatenate(picks, axis=0)


def dense_kernel(x, px, up, pup, v_in, u_in, bias, out, pooled, both, prod, v, u, held, held_p, in_sems, sems):
    n, width = x.shape
    core = lax.axis_index("c")
    loads = []
    for source, target in ((v_in, v), (u_in, u)):
        for k in range(2):
            rows = slice(k * 128, (k + 1) * 128)
            loads.append(
                pltpu.make_async_copy(source.at[rows], target.at[rows], in_sems.at[len(loads)])
            )
            loads[-1].start()
    both[:n] = x[...]
    both[n:] = px[...]
    prod[:n] = (x[...].astype(F32) * up[...].astype(F32)).astype(BF)
    prod[n:] = (px[...].astype(F32) * pup[...].astype(F32)).astype(BF)
    loads[0].wait()
    loads[1].wait()
    hid = nt(v[...], both[...]).astype(BF)
    loads[2].wait()
    loads[3].wait()
    hgr = nt(u[...], prod[...]).astype(BF)
    hid_own = own_rows(hid.astype(F32), core).astype(BF)
    hgr_own = own_rows(hgr.astype(F32), core).astype(BF)
    step = 1152
    copies = []
    for side, (left, right) in enumerate(((hid_own, prod), (hgr_own, both))):
        for k in range(width // step):
            total = mm(left, right[:, k * step : (k + 1) * step])
            cols = slice(side * width + k * step, side * width + (k + 1) * step)
            for i in range(NX):
                held[i, :, cols] = total[i * NJ : (i + 1) * NJ].astype(BF)
            copies.append(
                pltpu.make_async_copy(
                    held.at[:, :, cols], out.at[:, :, cols], sems.at[len(copies)]
                )
            )
            copies[-1].start()
    hid_s = hid.astype(F32).T.astype(BF)
    hgr_s = hgr.astype(F32).T.astype(BF)
    for pair in range(TABLES // 2):
        cols = slice(EMB + pair * 256, EMB + pair * 256 + 256)
        mixed = mm(hid_s, u[:, cols]) + bias[cols].reshape(1, 256)
        back = mm(hgr_s, v[:, cols])
        up_float = jnp.concatenate([up[:, cols], pup[:, cols]], axis=0).astype(F32)
        held_p[:, pair * 256 : pair * 256 + 256] = (up_float * (1.0 + mixed) + back).astype(BF)
    copies.append(pltpu.make_async_copy(held_p, pooled, sems.at[len(copies)]))
    copies[-1].start()
    for copy in copies:
        copy.wait()


def slots_of(placement, used, visit):
    for j in range(NJ):
        used[j] = 0
    for table in range(TABLES):
        owner = placement[table]
        slot = used[owner]
        used[owner] = slot + 1
        visit(table, owner, slot)


def count_kernel(placement, ids, counts, state, used):
    n = ids.shape[2]
    state[...] = ids[...].astype(I32)
    at = lax.broadcasted_iota(I32, (RANK // 2, n), 0)
    row = lax.rem(lax.axis_index("x") + (at // 8) % 4, NX) * 64 + at % 8
    row = row + lax.rem(lax.axis_index("y") + at // 32, NY) * 8 + lax.axis_index("c") * 32

    def count_rows(table, owner, slot):
        eight = state[owner]
        four = jnp.where(slot == 0, eight[:4], eight[4:])
        count = jnp.where(four[0:1] == row, 1.0, 0.0)
        for k in range(1, 4):
            count = count + jnp.where(four[k : k + 1] == row, 1.0, 0.0)
        counts[table] = count.astype(BF)

    slots_of(placement, used, count_rows)


def table_kernel(placement, mine, pooled, pids, *refs):
    outs, (theirs, state, used) = refs[:4], refs[4:]
    count_kernel(placement, pids, theirs, state, used)
    for table in range(TABLES):
        both = jnp.concatenate([mine[table], theirs[table]], axis=1)
        total = mm(both, pooled[:, table * EMB : (table + 1) * EMB])
        for d in range(NY):
            outs[d][table] = total[d * 32 : (d + 1) * 32].astype(outs[d].dtype)


def total_of(refs):
    total = refs[0][...].astype(F32)
    for ref in refs[1:]:
        total = total + ref[...].astype(F32)
    return total


def table_second(*refs):
    total = total_of(refs[:NY])
    for d in range(NX):
        refs[NY + d][...] = total[:, d * 8 : (d + 1) * 8].astype(refs[NY + d].dtype)


def cross_kernel(came, out, sums):
    for k in range(came.shape[2] // EMB):
        cols = slice(k * EMB, (k + 1) * EMB)
        total = came[0, :, cols].astype(F32)
        for i in range(1, NX):
            total = total + came[i, :, cols].astype(F32)
        sums[:, k] = total
    for j in range(NJ):
        out[j] = sums[j].astype(BF)


def route_kernel(placement, cross, *refs):
    came, out, (held, used, at) = refs[:NX], refs[NX], refs[NX + 1 :]
    for k in range(2 * NJ):
        at[k] = 0

    def note(table, owner, slot):
        at[2 * owner + slot] = table + 1

    slots_of(placement, used, note)
    held[0] = jnp.zeros((8, EMB), F32)
    held[1:] = total_of(came)
    for j in range(NJ):
        slots = [held[at[2 * j + s]] for s in range(2)]
        out[j, :16] = jnp.concatenate(slots, axis=0).astype(BF)
        out[j, 16:] = cross[j]


def last_kernel(came, cross, table):
    scale = 1.0 / math.sqrt(EMB * 256)
    total = came[0, 16:].astype(F32)
    for j in range(1, NJ):
        total = total + came[j, 16:].astype(F32)
    for k in range(cross.shape[1] // EMB):
        cross[:, k * EMB : (k + 1) * EMB] = total[k : k + 1] * scale
    for y in range(NY):
        rows = came[y * NZ, :16].astype(F32)
        for z in range(1, NZ):
            rows = rows + came[y * NZ + z, :16].astype(F32)
        for s in range(2):
            table[s, y * 8 : (y + 1) * 8] = rows[s * 8 : (s + 1) * 8]


def shift(chunks, axis):
    n = len(chunks)
    return [chunks[0]] + [
        lax.ppermute(chunks[d], axis, [(i, (i + d) % n) for i in range(n)]) for d in range(1, n)
    ]


def on_device(cross_input, upstream, v_weight, u_weight, bias, placement, owned_ids):
    samples, width = cross_input.shape
    blocks = 2 * width // EMB
    swap = [(0, 1), (1, 0)]
    px = lax.ppermute(cross_input, "c", swap)
    pup = lax.ppermute(upstream, "c", swap)

    (ids,) = call(ids_kernel, "ids", [((NJ, 8, EMB), I16)], owned_ids, specs=[VMEM], flops=40 << 30, size=60 << 20, vmem=4 << 20)
    ids = lax.all_to_all(ids, ("y", "z"), 0, 0, tiled=True)

    cross, pooled = call(
        dense_kernel,
        "dense",
        [((NX, NJ, 2 * width), BF), ((2 * samples, TABLES * EMB), BF)],
        cross_input,
        px,
        upstream,
        pup,
        v_weight,
        u_weight,
        bias,
        specs=[VMEM] * 4 + [HBM] * 2 + [VMEM],
        out_specs=[HBM] * 2,
        scratch=[pltpu.VMEM((2 * samples, width), BF)] * 2
        + [pltpu.VMEM((RANK, width), BF)] * 2
        + [
            pltpu.VMEM((NX, NJ, 2 * width), BF),
            pltpu.VMEM((2 * samples, TABLES * EMB), BF),
            pltpu.SemaphoreType.DMA((4,)),
            pltpu.SemaphoreType.DMA((7,)),
        ],
        vmem=50 << 20,
        flops=6 * 256 * 256 * width,
        size=6 << 20,
    )
    ids, cross = lax.optimization_barrier((ids, cross))
    cross = lax.all_to_all(cross, "x", 0, 0, tiled=True)
    pids = lax.ppermute(ids, "c", swap)

    counted = ((TABLES, RANK // 2, samples), BF)
    work = [pltpu.VMEM((NJ, 8, EMB), I32), pltpu.SMEM((NJ,), I32)]
    (counts,) = call(
        count_kernel,
        "counts",
        [counted],
        placement,
        ids,
        scratch=work,
        flops=1 << 30,
        size=1 << 20,
    )
    tables = call(
        table_kernel,
        "tables",
        [((TABLES, 32, EMB), F32)] + [((TABLES, 32, EMB), BF)] * 3,
        placement,
        counts,
        pooled,
        pids,
        scratch=[pltpu.VMEM(*counted)] + work,
        flops=6 * 256 * 256 * width,
        size=9 << 20,
    )
    tables = shift(tables, "y")
    tables = call(
        table_second,
        "table_second",
        [((TABLES, 8, EMB), F32)] + [((TABLES, 8, EMB), BF)] * 3,
        *tables,
        specs=[VMEM] * 4,
        size=1 << 20,
    )
    tables = shift(tables, "x")
    (cross,) = call(
        cross_kernel,
        "cross_sum",
        [((NJ, blocks, EMB), BF)],
        cross,
        specs=[VMEM],
        scratch=[pltpu.VMEM((NJ, blocks, EMB), F32)],
        size=3 << 20,
    )
    (routed,) = call(
        route_kernel,
        "route",
        [((NJ, 16 + blocks, EMB), BF)],
        placement,
        cross,
        *tables,
        scratch=[
            pltpu.VMEM((TABLES + 1, 8, EMB), F32),
            pltpu.SMEM((NJ,), I32),
            pltpu.SMEM((2 * NJ,), I32),
        ],
        size=2 << 20,
    )
    routed = lax.all_to_all(routed, ("y", "z"), 0, 0, tiled=True)
    return call(
        last_kernel,
        "last",
        [((1, 2 * width), F32), ((2, NJ, EMB), F32)],
        routed,
        specs=[VMEM],
        size=1 << 20,
    )


def solution(mesh):
    fine = Mesh(mesh.devices.reshape(NX, 2, NY, NZ), ("x", "c", "y", "z"))
    grp, tbl = ("x", "c"), ("y", "z")
    in_specs = (
        P(grp + tbl, None),
        P(grp + tbl, None),
        P(),
        P(),
        P(),
        P(),
        P(tbl, None, grp),
    )
    out_specs = (P(grp + tbl, None), P(tbl, grp, None))
    return jax.shard_map(
        on_device, mesh=fine, in_specs=in_specs, out_specs=out_specs, check_vma=False
    )
```

```python
import math

import jax
import jax.numpy as jnp
from jax import lax
from jax.experimental import pallas as pl
from jax.experimental.pallas import tpu as pltpu
from jax.sharding import Mesh
from jax.sharding import PartitionSpec as P

EMB = 128
TABLES = 26
RANK = 256
NX, NY, NZ = 4, 4, 8
NJ = NY * NZ
BF = jnp.bfloat16
F32 = jnp.float32
I32 = jnp.int32
I16 = jnp.int16

VMEM = pl.BlockSpec(memory_space=pltpu.VMEM)
SMEM = pl.BlockSpec(memory_space=pltpu.SMEM)
HBM = pl.BlockSpec(memory_space=pltpu.HBM)


def nt(left, right):
    return lax.dot_general(left, right, (((1,), (1,)), ((), ())), preferred_element_type=F32)


def mm(left, right):
    return jnp.dot(left, right, preferred_element_type=F32)


def call(kernel, name, outs, *args, specs=None, out_specs=None, scratch=(), flops=0, size=0, vmem=24 << 20):
    return pl.pallas_call(
        kernel,
        out_shape=tuple(jax.ShapeDtypeStruct(shape, dtype) for shape, dtype in outs),
        in_specs=specs or [SMEM] + [VMEM] * (len(args) - 1),
        out_specs=tuple(out_specs or [VMEM] * len(outs)),
        scratch_shapes=list(scratch),
        compiler_params=pltpu.CompilerParams(vmem_limit_bytes=vmem),
        cost_estimate=pl.CostEstimate(flops=flops, bytes_accessed=size, transcendentals=0),
        name=name,
    )(*args)


def ids_kernel(ids, out):
    for j in range(NJ):
        parts = [ids[s, :, j * EMB : (j + 1) * EMB] for s in range(2)]
        out[j] = jnp.concatenate(parts, axis=0).astype(I16)


def own_rows(full, core):
    picks = [
        jnp.where(core == 0, full[i * 64 : i * 64 + 32], full[i * 64 + 32 : i * 64 + 64])
        for i in range(NX)
    ]
    return jnp.concatenate(picks, axis=0)


def dense_kernel(x, px, up, pup, v_in, u_in, bias, out, pooled, both, prod, v, u, held, held_p, in_sems, sems):
    n, width = x.shape
    core = lax.axis_index("c")
    step = 1152
    copies = []

    def load(source, target, first):
        parts = [slice(k * 128, (k + 1) * 128) for k in range(2)]
        loads = [
            pltpu.make_async_copy(source.at[rows], target.at[rows], in_sems.at[first + k])
            for k, rows in enumerate(parts)
        ]
        for part in loads:
            part.start()
        return loads

    def send(source, target):
        copies.append(pltpu.make_async_copy(source, target, sems.at[len(copies)]))
        copies[-1].start()

    def half(left, right, base):
        for k in range(width // step):
            total = mm(left, right[:, k * step : (k + 1) * step])
            cols = slice(base + k * step, base + (k + 1) * step)
            for i in range(NX):
                held[i, :, cols] = total[i * NJ : (i + 1) * NJ].astype(BF)
            send(held.at[:, :, cols], out.at[:, :, cols])

    loads = load(v_in, v, 0)
    both[:n] = x[...]
    both[n:] = px[...]
    prod[:n] = (x[...].astype(F32) * up[...].astype(F32)).astype(BF)
    prod[n:] = (px[...].astype(F32) * pup[...].astype(F32)).astype(BF)
    for part in loads:
        part.wait()
    loads = load(u_in, u, 2)
    hid = nt(v[...], both[...]).astype(BF)
    half(own_rows(hid.astype(F32), core).astype(BF), prod, 0)
    for part in loads:
        part.wait()
    hgr = nt(u[...], prod[...]).astype(BF)
    half(own_rows(hgr.astype(F32), core).astype(BF), both, width)
    hid_s = hid.astype(F32).T.astype(BF)
    hgr_s = hgr.astype(F32).T.astype(BF)
    sent = 0
    for pair in range(TABLES // 2):
        cols = slice(EMB + pair * 256, EMB + pair * 256 + 256)
        mixed = mm(hid_s, u[:, cols]) + bias[cols].reshape(1, 256)
        back = mm(hgr_s, v[:, cols])
        up_float = jnp.concatenate([up[:, cols], pup[:, cols]], axis=0).astype(F32)
        held_p[:, pair * 256 : pair * 256 + 256] = (up_float * (1.0 + mixed) + back).astype(BF)
        if pair in (3, 7, 10, 12):
            cols = slice(sent, pair * 256 + 256)
            send(held_p.at[:, cols], pooled.at[:, cols])
            sent = pair * 256 + 256
    for copy in copies:
        copy.wait()


def slots_of(placement, used, visit):
    for j in range(NJ):
        used[j] = 0
    for table in range(TABLES):
        owner = placement[table]
        slot = used[owner]
        used[owner] = slot + 1
        visit(table, owner, slot)


def count_kernel(placement, ids, counts, state, used):
    n = ids.shape[2]
    state[...] = ids[...].astype(I32)
    at = lax.broadcasted_iota(I32, (RANK // 2, n), 0)
    row = lax.rem(lax.axis_index("x") + (at // 8) % 4, NX) * 64 + at % 8
    row = row + lax.rem(lax.axis_index("y") + at // 32, NY) * 8 + lax.axis_index("c") * 32

    def count_rows(table, owner, slot):
        eight = state[owner]
        four = jnp.where(slot == 0, eight[:4], eight[4:])
        count = jnp.where(four[0:1] == row, 1.0, 0.0)
        for k in range(1, 4):
            count = count + jnp.where(four[k : k + 1] == row, 1.0, 0.0)
        counts[table] = count.astype(BF)

    slots_of(placement, used, count_rows)


def table_kernel(placement, mine, pooled, pids, *refs):
    outs, (theirs, state, used) = refs[:4], refs[4:]
    count_kernel(placement, pids, theirs, state, used)
    for table in range(TABLES):
        both = jnp.concatenate([mine[table], theirs[table]], axis=1)
        total = mm(both, pooled[:, table * EMB : (table + 1) * EMB])
        for d in range(NY):
            outs[d][table] = total[d * 32 : (d + 1) * 32].astype(outs[d].dtype)


def total_of(refs):
    total = refs[0][...].astype(F32)
    for ref in refs[1:]:
        total = total + ref[...].astype(F32)
    return total


def table_second(*refs):
    total = total_of(refs[:NY])
    for d in range(NX):
        refs[NY + d][...] = total[:, d * 8 : (d + 1) * 8].astype(refs[NY + d].dtype)


def cross_kernel(came, out, sums):
    for k in range(came.shape[2] // EMB):
        cols = slice(k * EMB, (k + 1) * EMB)
        total = came[0, :, cols].astype(F32)
        for i in range(1, NX):
            total = total + came[i, :, cols].astype(F32)
        sums[:, k] = total
    for j in range(NJ):
        out[j] = sums[j].astype(BF)


def route_kernel(placement, cross, *refs):
    came, out, (held, used, at) = refs[:NX], refs[NX], refs[NX + 1 :]
    for k in range(2 * NJ):
        at[k] = 0

    def note(table, owner, slot):
        at[2 * owner + slot] = table + 1

    slots_of(placement, used, note)
    held[0] = jnp.zeros((8, EMB), F32)
    held[1:] = total_of(came)
    for j in range(NJ):
        slots = [held[at[2 * j + s]] for s in range(2)]
        out[j, :16] = jnp.concatenate(slots, axis=0).astype(BF)
        out[j, 16:] = cross[j]


def last_kernel(came, cross, table):
    scale = 1.0 / math.sqrt(EMB * 256)
    total = came[0, 16:].astype(F32)
    for j in range(1, NJ):
        total = total + came[j, 16:].astype(F32)
    for k in range(cross.shape[1] // EMB):
        cross[:, k * EMB : (k + 1) * EMB] = total[k : k + 1] * scale
    for y in range(NY):
        rows = came[y * NZ, :16].astype(F32)
        for z in range(1, NZ):
            rows = rows + came[y * NZ + z, :16].astype(F32)
        for s in range(2):
            table[s, y * 8 : (y + 1) * 8] = rows[s * 8 : (s + 1) * 8]


def shift(chunks, axis):
    n = len(chunks)
    return [chunks[0]] + [
        lax.ppermute(chunks[d], axis, [(i, (i + d) % n) for i in range(n)]) for d in range(1, n)
    ]


def on_device(cross_input, upstream, v_weight, u_weight, bias, placement, owned_ids):
    samples, width = cross_input.shape
    blocks = 2 * width // EMB
    swap = [(0, 1), (1, 0)]
    px = lax.ppermute(cross_input, "c", swap)
    pup = lax.ppermute(upstream, "c", swap)

    (ids,) = call(ids_kernel, "ids", [((NJ, 8, EMB), I16)], owned_ids, specs=[VMEM], flops=40 << 30, size=60 << 20, vmem=4 << 20)
    ids = lax.all_to_all(ids, ("y", "z"), 0, 0, tiled=True)

    cross, pooled = call(
        dense_kernel,
        "dense",
        [((NX, NJ, 2 * width), BF), ((2 * samples, TABLES * EMB), BF)],
        cross_input,
        px,
        upstream,
        pup,
        v_weight,
        u_weight,
        bias,
        specs=[VMEM] * 4 + [HBM] * 2 + [VMEM],
        out_specs=[HBM] * 2,
        scratch=[pltpu.VMEM((2 * samples, width), BF)] * 2
        + [pltpu.VMEM((RANK, width), BF)] * 2
        + [
            pltpu.VMEM((NX, NJ, 2 * width), BF),
            pltpu.VMEM((2 * samples, TABLES * EMB), BF),
            pltpu.SemaphoreType.DMA((4,)),
            pltpu.SemaphoreType.DMA((10,)),
        ],
        vmem=50 << 20,
        flops=6 * 256 * 256 * width,
        size=6 << 20,
    )
    ids, cross = lax.optimization_barrier((ids, cross))
    cross = lax.all_to_all(cross, "x", 0, 0, tiled=True)
    pids = lax.ppermute(ids, "c", swap)

    counted = ((TABLES, RANK // 2, samples), BF)
    work = [pltpu.VMEM((NJ, 8, EMB), I32), pltpu.SMEM((NJ,), I32)]
    (counts,) = call(
        count_kernel,
        "counts",
        [counted],
        placement,
        ids,
        scratch=work,
        flops=1 << 30,
        size=1 << 20,
    )
    tables = call(
        table_kernel,
        "tables",
        [((TABLES, 32, EMB), F32)] + [((TABLES, 32, EMB), BF)] * 3,
        placement,
        counts,
        pooled,
        pids,
        scratch=[pltpu.VMEM(*counted)] + work,
        flops=6 * 256 * 256 * width,
        size=9 << 20,
    )
    tables = shift(tables, "y")
    tables = call(
        table_second,
        "table_second",
        [((TABLES, 8, EMB), F32)] + [((TABLES, 8, EMB), BF)] * 3,
        *tables,
        specs=[VMEM] * 4,
        size=1 << 20,
    )
    tables = shift(tables, "x")
    (cross,) = call(
        cross_kernel,
        "cross_sum",
        [((NJ, blocks, EMB), BF)],
        cross,
        specs=[VMEM],
        scratch=[pltpu.VMEM((NJ, blocks, EMB), F32)],
        size=3 << 20,
    )
    (routed,) = call(
        route_kernel,
        "route",
        [((NJ, 16 + blocks, EMB), BF)],
        placement,
        cross,
        *tables,
        scratch=[
            pltpu.VMEM((TABLES + 1, 8, EMB), F32),
            pltpu.SMEM((NJ,), I32),
            pltpu.SMEM((2 * NJ,), I32),
        ],
        size=2 << 20,
    )
    routed = lax.all_to_all(routed, ("y", "z"), 0, 0, tiled=True)
    return call(
        last_kernel,
        "last",
        [((1, 2 * width), F32), ((2, NJ, EMB), F32)],
        routed,
        specs=[VMEM],
        size=1 << 20,
    )


def solution(mesh):
    fine = Mesh(mesh.devices.reshape(NX, 2, NY, NZ), ("x", "c", "y", "z"))
    grp, tbl = ("x", "c"), ("y", "z")
    in_specs = (
        P(grp + tbl, None),
        P(grp + tbl, None),
        P(),
        P(),
        P(),
        P(),
        P(tbl, None, grp),
    )
    out_specs = (P(grp + tbl, None), P(tbl, grp, None))
    return jax.shard_map(
        on_device, mesh=fine, in_specs=in_specs, out_specs=out_specs, check_vma=False
    )
```

```python
import math

import jax
import jax.numpy as jnp
from jax import lax
from jax.experimental import pallas as pl
from jax.experimental.pallas import tpu as pltpu
from jax.sharding import Mesh
from jax.sharding import PartitionSpec as P

EMB = 128
TABLES = 26
RANK = 256
NX, NY, NZ = 4, 4, 8
NJ = NY * NZ
BF = jnp.bfloat16
F32 = jnp.float32
I32 = jnp.int32
I16 = jnp.int16

VMEM = pl.BlockSpec(memory_space=pltpu.VMEM)
SMEM = pl.BlockSpec(memory_space=pltpu.SMEM)
HBM = pl.BlockSpec(memory_space=pltpu.HBM)


def nt(left, right):
    return lax.dot_general(left, right, (((1,), (1,)), ((), ())), preferred_element_type=F32)


def mm(left, right):
    return jnp.dot(left, right, preferred_element_type=F32)


def call(kernel, name, outs, *args, specs=None, out_specs=None, scratch=(), flops=0, size=0, vmem=24 << 20):
    return pl.pallas_call(
        kernel,
        out_shape=tuple(jax.ShapeDtypeStruct(shape, dtype) for shape, dtype in outs),
        in_specs=specs or [SMEM] + [VMEM] * (len(args) - 1),
        out_specs=tuple(out_specs or [VMEM] * len(outs)),
        scratch_shapes=list(scratch),
        compiler_params=pltpu.CompilerParams(vmem_limit_bytes=vmem),
        cost_estimate=pl.CostEstimate(flops=flops, bytes_accessed=size, transcendentals=0),
        name=name,
    )(*args)


def ids_kernel(ids, out):
    for j in range(NJ):
        parts = [ids[s, :, j * EMB : (j + 1) * EMB] for s in range(2)]
        out[j] = jnp.concatenate(parts, axis=0).astype(I16)


def own_rows(full, core):
    picks = [
        jnp.where(core == 0, full[i * 64 : i * 64 + 32], full[i * 64 + 32 : i * 64 + 64])
        for i in range(NX)
    ]
    return jnp.concatenate(picks, axis=0)


def dense_kernel(v, x, px, up, pup_in, u_in, bias, out, pooled, both, prod, pup, u, held, held_p, in_sems, sems):
    n, width = x.shape
    core = lax.axis_index("c")
    step = 1152
    copies = []

    def load(source, target, first):
        parts = [slice(k * 128, (k + 1) * 128) for k in range(2)]
        loads = [
            pltpu.make_async_copy(source.at[rows], target.at[rows], in_sems.at[first + k])
            for k, rows in enumerate(parts)
        ]
        for part in loads:
            part.start()
        return loads

    def send(source, target):
        copies.append(pltpu.make_async_copy(source, target, sems.at[len(copies)]))
        copies[-1].start()

    def half(left, right, base):
        for k in range(width // step):
            total = mm(left, right[:, k * step : (k + 1) * step])
            cols = slice(base + k * step, base + (k + 1) * step)
            for i in range(NX):
                held[i, :, cols] = total[i * NJ : (i + 1) * NJ].astype(BF)
            send(held.at[:, :, cols], out.at[:, :, cols])

    loads = [
        pltpu.make_async_copy(px, both.at[n:], in_sems.at[2]),
        pltpu.make_async_copy(pup_in, pup, in_sems.at[3]),
    ]
    for part in loads:
        part.start()
    later = load(u_in, u, 0)
    both[:n] = x[...]
    prod[:n] = (x[...].astype(F32) * up[...].astype(F32)).astype(BF)
    hid_x = nt(v[...], x[...])
    loads[0].wait()
    hid = jnp.concatenate([hid_x, nt(v[...], both[n:])], axis=1).astype(BF)
    loads[1].wait()
    prod[n:] = (both[n:].astype(F32) * pup[...].astype(F32)).astype(BF)
    half(own_rows(hid.astype(F32), core).astype(BF), prod, 0)
    for part in later:
        part.wait()
    hgr = nt(u[...], prod[...]).astype(BF)
    half(own_rows(hgr.astype(F32), core).astype(BF), both, width)
    hid_s = hid.astype(F32).T.astype(BF)
    hgr_s = hgr.astype(F32).T.astype(BF)
    sent = 0
    for pair in range(TABLES // 2):
        cols = slice(EMB + pair * 256, EMB + pair * 256 + 256)
        mixed = mm(hid_s, u[:, cols]) + bias[cols].reshape(1, 256)
        back = mm(hgr_s, v[:, cols])
        up_float = jnp.concatenate([up[:, cols], pup[:, cols]], axis=0).astype(F32)
        held_p[:, pair * 256 : pair * 256 + 256] = (up_float * (1.0 + mixed) + back).astype(BF)
        if pair in (3, 7, 10, 12):
            cols = slice(sent, pair * 256 + 256)
            send(held_p.at[:, cols], pooled.at[:, cols])
            sent = pair * 256 + 256
    for copy in copies:
        copy.wait()


def slots_of(placement, used, visit):
    for j in range(NJ):
        used[j] = 0
    for table in range(TABLES):
        owner = placement[table]
        slot = used[owner]
        used[owner] = slot + 1
        visit(table, owner, slot)


def count_kernel(placement, ids, counts, state, used):
    n = ids.shape[2]
    state[...] = ids[...].astype(I32)
    at = lax.broadcasted_iota(I32, (RANK // 2, n), 0)
    row = lax.rem(lax.axis_index("x") + (at // 8) % 4, NX) * 64 + at % 8
    row = row + lax.rem(lax.axis_index("y") + at // 32, NY) * 8 + lax.axis_index("c") * 32

    def count_rows(table, owner, slot):
        eight = state[owner]
        four = jnp.where(slot == 0, eight[:4], eight[4:])
        count = jnp.where(four[0:1] == row, 1.0, 0.0)
        for k in range(1, 4):
            count = count + jnp.where(four[k : k + 1] == row, 1.0, 0.0)
        counts[table] = count.astype(BF)

    slots_of(placement, used, count_rows)


def table_kernel(placement, mine, pooled, pids, *refs):
    outs, (theirs, state, used) = refs[:4], refs[4:]
    count_kernel(placement, pids, theirs, state, used)
    for table in range(TABLES):
        both = jnp.concatenate([mine[table], theirs[table]], axis=1)
        total = mm(both, pooled[:, table * EMB : (table + 1) * EMB])
        for d in range(NY):
            outs[d][table] = total[d * 32 : (d + 1) * 32].astype(outs[d].dtype)


def total_of(refs):
    total = refs[0][...].astype(F32)
    for ref in refs[1:]:
        total = total + ref[...].astype(F32)
    return total


def table_second(*refs):
    total = total_of(refs[:NY])
    for d in range(NX):
        refs[NY + d][...] = total[:, d * 8 : (d + 1) * 8].astype(refs[NY + d].dtype)


def cross_kernel(came, out, sums):
    for k in range(came.shape[2] // EMB):
        cols = slice(k * EMB, (k + 1) * EMB)
        total = came[0, :, cols].astype(F32)
        for i in range(1, NX):
            total = total + came[i, :, cols].astype(F32)
        sums[:, k] = total
    for j in range(NJ):
        out[j] = sums[j].astype(BF)


def route_kernel(placement, cross, *refs):
    came, out, (held, used, at) = refs[:NX], refs[NX], refs[NX + 1 :]
    for k in range(2 * NJ):
        at[k] = 0

    def note(table, owner, slot):
        at[2 * owner + slot] = table + 1

    slots_of(placement, used, note)
    held[0] = jnp.zeros((8, EMB), F32)
    held[1:] = total_of(came)
    for j in range(NJ):
        slots = [held[at[2 * j + s]] for s in range(2)]
        out[j, :16] = jnp.concatenate(slots, axis=0).astype(BF)
        out[j, 16:] = cross[j]


def last_kernel(came, cross, table):
    scale = 1.0 / math.sqrt(EMB * 256)
    total = came[0, 16:].astype(F32)
    for j in range(1, NJ):
        total = total + came[j, 16:].astype(F32)
    for k in range(cross.shape[1] // EMB):
        cross[:, k * EMB : (k + 1) * EMB] = total[k : k + 1] * scale
    for y in range(NY):
        rows = came[y * NZ, :16].astype(F32)
        for z in range(1, NZ):
            rows = rows + came[y * NZ + z, :16].astype(F32)
        for s in range(2):
            table[s, y * 8 : (y + 1) * 8] = rows[s * 8 : (s + 1) * 8]


def shift(chunks, axis):
    n = len(chunks)
    return [chunks[0]] + [
        lax.ppermute(chunks[d], axis, [(i, (i + d) % n) for i in range(n)]) for d in range(1, n)
    ]


def on_device(cross_input, upstream, v_weight, u_weight, bias, placement, owned_ids):
    samples, width = cross_input.shape
    blocks = 2 * width // EMB
    swap = [(0, 1), (1, 0)]
    px = lax.ppermute(cross_input, "c", swap)
    pup = lax.ppermute(upstream, "c", swap)

    (ids,) = call(ids_kernel, "ids", [((NJ, 8, EMB), I16)], owned_ids, specs=[VMEM], flops=40 << 30, size=60 << 20, vmem=4 << 20)
    ids = lax.all_to_all(ids, ("y", "z"), 0, 0, tiled=True)

    cross, pooled = call(
        dense_kernel,
        "dense",
        [((NX, NJ, 2 * width), BF), ((2 * samples, TABLES * EMB), BF)],
        v_weight,
        cross_input,
        px,
        upstream,
        pup,
        u_weight,
        bias,
        specs=[VMEM, VMEM, HBM, VMEM, HBM, HBM, VMEM],
        out_specs=[HBM] * 2,
        scratch=[pltpu.VMEM((2 * samples, width), BF)] * 2
        + [pltpu.VMEM((samples, width), BF), pltpu.VMEM((RANK, width), BF)]
        + [
            pltpu.VMEM((NX, NJ, 2 * width), BF),
            pltpu.VMEM((2 * samples, TABLES * EMB), BF),
            pltpu.SemaphoreType.DMA((4,)),
            pltpu.SemaphoreType.DMA((10,)),
        ],
        vmem=45 << 20,
        flops=6 * 256 * 256 * width,
        size=6 << 20,
    )
    ids, cross = lax.optimization_barrier((ids, cross))
    cross = lax.all_to_all(cross, "x", 0, 0, tiled=True)
    pids = lax.ppermute(ids, "c", swap)

    counted = ((TABLES, RANK // 2, samples), BF)
    work = [pltpu.VMEM((NJ, 8, EMB), I32), pltpu.SMEM((NJ,), I32)]
    (counts,) = call(
        count_kernel,
        "counts",
        [counted],
        placement,
        ids,
        scratch=work,
        flops=1 << 30,
        size=1 << 20,
    )
    tables = call(
        table_kernel,
        "tables",
        [((TABLES, 32, EMB), F32)] + [((TABLES, 32, EMB), BF)] * 3,
        placement,
        counts,
        pooled,
        pids,
        scratch=[pltpu.VMEM(*counted)] + work,
        flops=6 * 256 * 256 * width,
        size=9 << 20,
    )
    tables = shift(tables, "y")
    tables = call(
        table_second,
        "table_second",
        [((TABLES, 8, EMB), F32)] + [((TABLES, 8, EMB), BF)] * 3,
        *tables,
        specs=[VMEM] * 4,
        size=1 << 20,
    )
    tables = shift(tables, "x")
    (cross,) = call(
        cross_kernel,
        "cross_sum",
        [((NJ, blocks, EMB), BF)],
        cross,
        specs=[VMEM],
        scratch=[pltpu.VMEM((NJ, blocks, EMB), F32)],
        size=3 << 20,
    )
    (routed,) = call(
        route_kernel,
        "route",
        [((NJ, 16 + blocks, EMB), BF)],
        placement,
        cross,
        *tables,
        scratch=[
            pltpu.VMEM((TABLES + 1, 8, EMB), F32),
            pltpu.SMEM((NJ,), I32),
            pltpu.SMEM((2 * NJ,), I32),
        ],
        size=2 << 20,
    )
    routed = lax.all_to_all(routed, ("y", "z"), 0, 0, tiled=True)
    return call(
        last_kernel,
        "last",
        [((1, 2 * width), F32), ((2, NJ, EMB), F32)],
        routed,
        specs=[VMEM],
        size=1 << 20,
    )


def solution(mesh):
    fine = Mesh(mesh.devices.reshape(NX, 2, NY, NZ), ("x", "c", "y", "z"))
    grp, tbl = ("x", "c"), ("y", "z")
    in_specs = (
        P(grp + tbl, None),
        P(grp + tbl, None),
        P(),
        P(),
        P(),
        P(),
        P(tbl, None, grp),
    )
    out_specs = (P(grp + tbl, None), P(tbl, grp, None))
    return jax.shard_map(
        on_device, mesh=fine, in_specs=in_specs, out_specs=out_specs, check_vma=False
    )
```

```python
import math

import jax
import jax.numpy as jnp
from jax import lax
from jax.experimental import pallas as pl
from jax.experimental.pallas import tpu as pltpu
from jax.sharding import Mesh
from jax.sharding import PartitionSpec as P

EMB = 128
TABLES = 26
RANK = 256
NX, NY, NZ = 4, 4, 8
NJ = NY * NZ
BF = jnp.bfloat16
F32 = jnp.float32
I32 = jnp.int32
I16 = jnp.int16

VMEM = pl.BlockSpec(memory_space=pltpu.VMEM)
SMEM = pl.BlockSpec(memory_space=pltpu.SMEM)
HBM = pl.BlockSpec(memory_space=pltpu.HBM)


def nt(left, right):
    return lax.dot_general(left, right, (((1,), (1,)), ((), ())), preferred_element_type=F32)


def mm(left, right):
    return jnp.dot(left, right, preferred_element_type=F32)


def call(kernel, name, outs, *args, specs=None, out_specs=None, scratch=(), flops=0, size=0, vmem=24 << 20):
    return pl.pallas_call(
        kernel,
        out_shape=tuple(jax.ShapeDtypeStruct(shape, dtype) for shape, dtype in outs),
        in_specs=specs or [SMEM] + [VMEM] * (len(args) - 1),
        out_specs=tuple(out_specs or [VMEM] * len(outs)),
        scratch_shapes=list(scratch),
        compiler_params=pltpu.CompilerParams(vmem_limit_bytes=vmem),
        cost_estimate=pl.CostEstimate(flops=flops, bytes_accessed=size, transcendentals=0),
        name=name,
    )(*args)


def ids_kernel(ids, out):
    for j in range(NJ):
        parts = [ids[s, :, j * EMB : (j + 1) * EMB] for s in range(2)]
        out[j] = jnp.concatenate(parts, axis=0).astype(I16)


def own_rows(full, core):
    picks = [
        jnp.where(core == 0, full[i * 64 : i * 64 + 32], full[i * 64 + 32 : i * 64 + 64])
        for i in range(NX)
    ]
    return jnp.concatenate(picks, axis=0)


def dense_kernel(x, px, up, pup, v_in, u_in, bias, out, pooled, both, prod, v, u, held, held_p, in_sems, sems):
    n, width = x.shape
    core = lax.axis_index("c")
    step = 1152
    copies = []

    def load(source, target, first):
        parts = [slice(k * 128, (k + 1) * 128) for k in range(2)]
        loads = [
            pltpu.make_async_copy(source.at[rows], target.at[rows], in_sems.at[first + k])
            for k, rows in enumerate(parts)
        ]
        for part in loads:
            part.start()
        return loads

    def send(source, target):
        copies.append(pltpu.make_async_copy(source, target, sems.at[len(copies)]))
        copies[-1].start()

    def half(left, right, base):
        for k in range(width // step):
            total = mm(left, right[:, k * step : (k + 1) * step])
            cols = slice(base + k * step, base + (k + 1) * step)
            for i in range(NX):
                held[i, :, cols] = total[i * NJ : (i + 1) * NJ].astype(BF)
            send(held.at[:, :, cols], out.at[:, :, cols])

    loads = load(v_in, v, 0)
    both[:n] = x[...]
    both[n:] = px[...]
    prod[:n] = (x[...].astype(F32) * up[...].astype(F32)).astype(BF)
    prod[n:] = (px[...].astype(F32) * pup[...].astype(F32)).astype(BF)
    for part in loads:
        part.wait()
    loads = load(u_in, u, 2)
    hid = nt(v[...], both[...]).astype(BF)
    half(own_rows(hid.astype(F32), core).astype(BF), prod, 0)
    for part in loads:
        part.wait()
    hgr = nt(u[...], prod[...]).astype(BF)
    half(own_rows(hgr.astype(F32), core).astype(BF), both, width)
    hid_s = hid.astype(F32).T.astype(BF)
    hgr_s = hgr.astype(F32).T.astype(BF)
    sent = 0
    for pair in range(TABLES // 2):
        cols = slice(EMB + pair * 256, EMB + pair * 256 + 256)
        mixed = mm(hid_s, u[:, cols]) + bias[cols].reshape(1, 256)
        back = mm(hgr_s, v[:, cols])
        up_float = jnp.concatenate([up[:, cols], pup[:, cols]], axis=0).astype(F32)
        held_p[:, pair * 256 : pair * 256 + 256] = (up_float * (1.0 + mixed) + back).astype(BF)
        if pair in (3, 7, 10, 12):
            cols = slice(sent, pair * 256 + 256)
            send(held_p.at[:, cols], pooled.at[:, cols])
            sent = pair * 256 + 256
    for copy in copies:
        copy.wait()


def slots_of(placement, used, visit):
    for j in range(NJ):
        used[j] = 0
    for table in range(TABLES):
        owner = placement[table]
        slot = used[owner]
        used[owner] = slot + 1
        visit(table, owner, slot)


def count_kernel(placement, ids, counts, state, used):
    n = ids.shape[2]
    state[...] = ids[...].astype(I32)
    at = lax.broadcasted_iota(I32, (RANK // 2, n), 0)
    row = lax.rem(lax.axis_index("x") + (at // 8) % 4, NX) * 64 + at % 8
    row = row + lax.rem(lax.axis_index("y") + at // 32, NY) * 8 + lax.axis_index("c") * 32
    row = row.astype(F32).astype(BF)

    def count_rows(table, owner, slot):
        eight = state[owner]
        four = jnp.where(slot == 0, eight[:4], eight[4:]).astype(F32).astype(BF)
        one, none = jnp.ones(row.shape, BF), jnp.zeros(row.shape, BF)
        count = jnp.where(four[0:1] == row, one, none)
        for k in range(1, 4):
            count = count + jnp.where(four[k : k + 1] == row, one, none)
        counts[table] = count

    slots_of(placement, used, count_rows)


def table_kernel(placement, mine, pooled, pids, *refs):
    outs, (theirs, state, used) = refs[:4], refs[4:]
    count_kernel(placement, pids, theirs, state, used)
    for table in range(TABLES):
        both = jnp.concatenate([mine[table], theirs[table]], axis=1)
        total = mm(both, pooled[:, table * EMB : (table + 1) * EMB])
        for d in range(NY):
            outs[d][table] = total[d * 32 : (d + 1) * 32].astype(outs[d].dtype)


def total_of(refs):
    total = refs[0][...].astype(F32)
    for ref in refs[1:]:
        total = total + ref[...].astype(F32)
    return total


def table_second(*refs):
    total = total_of(refs[:NY])
    for d in range(NX):
        refs[NY + d][...] = total[:, d * 8 : (d + 1) * 8].astype(refs[NY + d].dtype)


def cross_kernel(came, out, sums):
    for k in range(came.shape[2] // EMB):
        cols = slice(k * EMB, (k + 1) * EMB)
        total = came[0, :, cols].astype(F32)
        for i in range(1, NX):
            total = total + came[i, :, cols].astype(F32)
        sums[:, k] = total
    for j in range(NJ):
        out[j] = sums[j].astype(BF)


def route_kernel(placement, cross, *refs):
    came, out, (held, used, at) = refs[:NX], refs[NX], refs[NX + 1 :]
    for k in range(2 * NJ):
        at[k] = 0

    def note(table, owner, slot):
        at[2 * owner + slot] = table + 1

    slots_of(placement, used, note)
    held[0] = jnp.zeros((8, EMB), F32)
    held[1:] = total_of(came)
    for j in range(NJ):
        slots = [held[at[2 * j + s]] for s in range(2)]
        out[j, :16] = jnp.concatenate(slots, axis=0).astype(BF)
        out[j, 16:] = cross[j]


def last_kernel(came, cross, table):
    scale = 1.0 / math.sqrt(EMB * 256)
    total = came[0, 16:].astype(F32)
    for j in range(1, NJ):
        total = total + came[j, 16:].astype(F32)
    for k in range(cross.shape[1] // EMB):
        cross[:, k * EMB : (k + 1) * EMB] = total[k : k + 1] * scale
    for y in range(NY):
        rows = came[y * NZ, :16].astype(F32)
        for z in range(1, NZ):
            rows = rows + came[y * NZ + z, :16].astype(F32)
        for s in range(2):
            table[s, y * 8 : (y + 1) * 8] = rows[s * 8 : (s + 1) * 8]


def shift(chunks, axis):
    n = len(chunks)
    return [chunks[0]] + [
        lax.ppermute(chunks[d], axis, [(i, (i + d) % n) for i in range(n)]) for d in range(1, n)
    ]


def on_device(cross_input, upstream, v_weight, u_weight, bias, placement, owned_ids):
    samples, width = cross_input.shape
    blocks = 2 * width // EMB
    swap = [(0, 1), (1, 0)]
    px = lax.ppermute(cross_input, "c", swap)
    pup = lax.ppermute(upstream, "c", swap)

    (ids,) = call(ids_kernel, "ids", [((NJ, 8, EMB), I16)], owned_ids, specs=[VMEM], flops=40 << 30, size=60 << 20, vmem=4 << 20)
    ids = lax.all_to_all(ids, ("y", "z"), 0, 0, tiled=True)

    cross, pooled = call(
        dense_kernel,
        "dense",
        [((NX, NJ, 2 * width), BF), ((2 * samples, TABLES * EMB), BF)],
        cross_input,
        px,
        upstream,
        pup,
        v_weight,
        u_weight,
        bias,
        specs=[VMEM] * 4 + [HBM] * 2 + [VMEM],
        out_specs=[HBM] * 2,
        scratch=[pltpu.VMEM((2 * samples, width), BF)] * 2
        + [pltpu.VMEM((RANK, width), BF)] * 2
        + [
            pltpu.VMEM((NX, NJ, 2 * width), BF),
            pltpu.VMEM((2 * samples, TABLES * EMB), BF),
            pltpu.SemaphoreType.DMA((4,)),
            pltpu.SemaphoreType.DMA((10,)),
        ],
        vmem=50 << 20,
        flops=6 * 256 * 256 * width,
        size=6 << 20,
    )
    ids, cross = lax.optimization_barrier((ids, cross))
    cross = lax.all_to_all(cross, "x", 0, 0, tiled=True)
    pids = lax.ppermute(ids, "c", swap)

    counted = ((TABLES, RANK // 2, samples), BF)
    work = [pltpu.VMEM((NJ, 8, EMB), I32), pltpu.SMEM((NJ,), I32)]
    (counts,) = call(
        count_kernel,
        "counts",
        [counted],
        placement,
        ids,
        scratch=work,
        flops=1 << 30,
        size=1 << 20,
    )
    tables = call(
        table_kernel,
        "tables",
        [((TABLES, 32, EMB), F32)] + [((TABLES, 32, EMB), BF)] * 3,
        placement,
        counts,
        pooled,
        pids,
        scratch=[pltpu.VMEM(*counted)] + work,
        flops=6 * 256 * 256 * width,
        size=9 << 20,
    )
    tables = shift(tables, "y")
    tables = call(
        table_second,
        "table_second",
        [((TABLES, 8, EMB), F32)] + [((TABLES, 8, EMB), BF)] * 3,
        *tables,
        specs=[VMEM] * 4,
        size=1 << 20,
    )
    tables = shift(tables, "x")
    (cross,) = call(
        cross_kernel,
        "cross_sum",
        [((NJ, blocks, EMB), BF)],
        cross,
        specs=[VMEM],
        scratch=[pltpu.VMEM((NJ, blocks, EMB), F32)],
        size=3 << 20,
    )
    (routed,) = call(
        route_kernel,
        "route",
        [((NJ, 16 + blocks, EMB), BF)],
        placement,
        cross,
        *tables,
        scratch=[
            pltpu.VMEM((TABLES + 1, 8, EMB), F32),
            pltpu.SMEM((NJ,), I32),
            pltpu.SMEM((2 * NJ,), I32),
        ],
        size=2 << 20,
    )
    routed = lax.all_to_all(routed, ("y", "z"), 0, 0, tiled=True)
    return call(
        last_kernel,
        "last",
        [((1, 2 * width), F32), ((2, NJ, EMB), F32)],
        routed,
        specs=[VMEM],
        size=1 << 20,
    )


def solution(mesh):
    fine = Mesh(mesh.devices.reshape(NX, 2, NY, NZ), ("x", "c", "y", "z"))
    grp, tbl = ("x", "c"), ("y", "z")
    in_specs = (
        P(grp + tbl, None),
        P(grp + tbl, None),
        P(),
        P(),
        P(),
        P(),
        P(tbl, None, grp),
    )
    out_specs = (P(grp + tbl, None), P(tbl, grp, None))
    return jax.shard_map(
        on_device, mesh=fine, in_specs=in_specs, out_specs=out_specs, check_vma=False
    )
```
